32 devices in a mesh: src: 4 (over x, core), tgt: 8 (over z, y).
Axes of the slice: x: 2, y: 2, z: 4, core: 2. Of those that a mesh axis runs over, the one named last changes fastest.
Arguments:
- src_feats: bfloat16 [32, 2560], P(None, ('src', 'tgt')), may hold values from -7 to 7
- src_factor: bfloat16 [16, 2560], P(None, ('src', 'tgt')), may hold values from 0.1 to 8
- tgt_feats: bfloat16 [32, 4096], P(None, ('tgt', 'src')), may hold values from -7 to 7
- tgt_factor: bfloat16 [16, 4096], P(None, ('tgt', 'src')), may hold values from 0.1 to 8
- rank_weight: float32 [16], replicated, may hold values from 0.5 to 4
Outputs:
- grad_src_feats: float32 [32, 2560], P(None, ('src', 'tgt'))
- grad_src_factor: float32 [16, 2560], P(None, ('src', 'tgt'))
- grad_tgt_feats: float32 [32, 4096], P(None, ('tgt', 'src'))
- grad_tgt_factor: float32 [16, 4096], P(None, ('tgt', 'src'))
The draws below stay inside these ranges and needn't reach their ends.
All inputs are finite; a program needn't handle non-finite values.
Results may differ from the reference program's by a relative error of at most 0.0015.
Values may be sent and summed in bfloat16 or wider, within the bound.
A program may use at most 64 MiB of HBM per device.

```python
import math
import jax
import jax.numpy as jnp
from jax import lax

F = 32
RANK = 16
TGT_DEV = 128
N = 2560
M = 4096
N_SRC = 4


coarse_total = 8


fine_total = 256


heavy_factor = 8.0


def scan_points(key, point_count, salt_value):
    coarse_key = jax.random.fold_in(key, 101)
    detail_key = jax.random.fold_in(key, 202)
    coarse = jax.random.uniform(coarse_key, (coarse_total, F), jnp.float32, -4.0, 4.0)
    offsets = jax.random.uniform(detail_key, (fine_total, F), jnp.float32, -1.4, 1.4)
    parent = jnp.arange(fine_total, dtype=jnp.int32) // (fine_total // coarse_total)
    centres = coarse[parent] + offsets
    point_key = jax.random.fold_in(key, salt_value)
    assign = jax.random.randint(jax.random.fold_in(point_key, 1), (point_count,), 0, fine_total)
    log_scale = jax.random.uniform(jax.random.fold_in(point_key, 2), (point_count, 1), jnp.float32, jnp.log(0.1), jnp.log(0.8))
    jitter = jax.random.uniform(jax.random.fold_in(point_key, 3), (point_count, F), jnp.float32, -1.0, 1.0)
    jitter = jitter * (1.7320508 * jnp.exp(log_scale))
    points = centres[assign] + jitter
    return jnp.transpose(points).astype(jnp.bfloat16)


def draw_src_feats(key, part):
    return scan_points(key, N, 11)


def draw_tgt_feats(key, part):
    return scan_points(key, M, 12)


def base_factor(key, point_count):
    return jnp.exp(jax.random.uniform(key, (RANK, point_count), jnp.float32, jnp.log(0.1), jnp.log(1.0)))


def draw_src_factor(key, part):
    base = base_factor(jax.random.fold_in(key, 301), N)
    chosen = jax.random.randint(jax.random.fold_in(key, 302), (N,), 0, RANK)
    rows = jnp.arange(RANK, dtype=jnp.int32)[:, None]
    boost = jnp.where(rows == chosen[None, :], heavy_factor, 1.0)
    return (base * boost).astype(jnp.bfloat16)


def draw_tgt_factor(key, part):
    base = base_factor(jax.random.fold_in(key, 401), M)
    column = jnp.arange(M, dtype=jnp.int32)
    tgt_index = column // TGT_DEV // N_SRC
    rows = jnp.arange(RANK, dtype=jnp.int32)[:, None]
    boost = jnp.where(rows == (tgt_index % RANK)[None, :], heavy_factor, 1.0)
    return (base * boost).astype(jnp.bfloat16)


def setup_inputs(seed: int = 0) -> dict:
    splits = jax.random.split(jax.random.key(seed), 6)
    src_feats = draw_src_feats(jax.random.fold_in(splits[5], 71), 0)
    src_factor = draw_src_factor(jax.random.fold_in(splits[5], 71), 0)
    tgt_feats = draw_tgt_feats(jax.random.fold_in(splits[5], 71), 0)
    tgt_factor = draw_tgt_factor(jax.random.fold_in(splits[5], 71), 0)
    rank_weight = jnp.clip(jnp.exp(jax.random.uniform(splits[4], (RANK,), jnp.float32, math.log(0.5), math.log(4.0))), 0.5, 4.0)
    return dict(src_feats=src_feats, src_factor=src_factor, tgt_feats=tgt_feats, tgt_factor=tgt_factor, rank_weight=rank_weight)


def tile_terms(src_x, src_q, tgt_y, scaled_r, inverse_g):
    sq_src = lax.optimization_barrier(jnp.sum(jnp.square(src_x.astype(jnp.float32)), 0))
    sq_tgt = lax.optimization_barrier(jnp.sum(jnp.square(tgt_y.astype(jnp.float32)), 0))
    inner_prod = jnp.dot(src_x.T, tgt_y, preferred_element_type=jnp.float32)
    distance = jnp.sqrt(sq_src[:, None] + sq_tgt[None, :] - 2.0 * inner_prod + 1.0)
    plan_tile = jnp.dot(src_q.T, scaled_r, preferred_element_type=jnp.float32)
    weight = (plan_tile / distance).astype(jnp.bfloat16)
    cost_bf = distance.astype(jnp.bfloat16)
    row_mass = lax.optimization_barrier(jnp.sum(weight.astype(jnp.float32), 1))
    col_mass = lax.optimization_barrier(jnp.sum(weight.astype(jnp.float32), 0))
    grad_x = src_x.astype(jnp.float32) * row_mass[None, :] - jnp.dot(tgt_y, weight.T, preferred_element_type=jnp.float32)
    grad_q = jnp.dot(scaled_r, cost_bf.T, preferred_element_type=jnp.float32)
    grad_y = tgt_y.astype(jnp.float32) * col_mass[None, :] - jnp.dot(src_x, weight, preferred_element_type=jnp.float32)
    grad_r = inverse_g[:, None] * jnp.dot(src_q, cost_bf, preferred_element_type=jnp.float32)
    return (jnp.concatenate([grad_x, grad_q], 0), jnp.concatenate([grad_y, grad_r], 0))

def reference(src_feats, src_factor, tgt_feats, tgt_factor, rank_weight):
    inverse_g = 1.0 / rank_weight
    scaled_r = (tgt_factor.astype(jnp.float32) * inverse_g[:, None]).astype(jnp.bfloat16)
    feature_count = src_feats.shape[0]
    total_src = src_feats.shape[1]
    total_tgt = tgt_feats.shape[1]
    block_rows = 512 if total_src % 512 == 0 else total_src
    block_count = total_src // block_rows

    def advance(totals, block_index):
        offset = (block_index * block_rows).astype(jnp.int32)
        src_x = lax.dynamic_slice_in_dim(src_feats, offset, block_rows, 1)
        src_q = lax.dynamic_slice_in_dim(src_factor, offset, block_rows, 1)
        src_part, tgt_part = tile_terms(src_x, src_q, tgt_feats, scaled_r, inverse_g)
        return (totals + tgt_part, src_part)
    start_totals = jnp.zeros((feature_count + src_factor.shape[0], total_tgt), jnp.float32)
    tgt_sum, src_blocks = lax.scan(advance, start_totals, jnp.arange(block_count, dtype=jnp.int32))
    src_sum = jnp.transpose(src_blocks, (1, 0, 2)).reshape(feature_count + src_factor.shape[0], total_src)
    scale = 1.0 / total_tgt
    return (src_sum[:feature_count] * scale, src_sum[feature_count:] * scale, tgt_sum[:feature_count] * scale, tgt_sum[feature_count:] * scale)
```

```python
import functools

import jax
import jax.numpy as jnp
from jax import lax
from jax.experimental import pallas as pl
from jax.experimental.pallas import tpu as pltpu
from jax.sharding import PartitionSpec as P

MESH = pl.DeviceIdType.MESH
NT = (((1,), (1,)), ((), ()))
AUG = 16


def each(low, high, body):
    if high - low <= 8:
        for i in range(low, high):
            body(i)
    else:
        lax.fori_loop(low, high, lambda i, c: (body(i), c)[1], 0)


def split3(value):
    high = value.astype(jnp.bfloat16).astype(jnp.float32)
    rest = value - high
    mid = rest.astype(jnp.bfloat16).astype(jnp.float32)
    return high, mid, rest - mid


def aug_rows(feats, first, ones_at, extra):
    wide = feats.astype(jnp.float32)
    norm = jnp.sum(wide * wide, axis=0, keepdims=True) + extra
    high, mid, low = split3(norm)
    shape = (AUG, feats.shape[1])
    row = lax.broadcasted_iota(jnp.int32, shape, 0)
    out = jnp.where((row >= ones_at) & (row < ones_at + 3), 1.0, 0.0)
    for k, part in enumerate((high, mid, low)):
        out = jnp.where(row == first + k, jnp.broadcast_to(part, shape), out)
    return out.astype(jnp.bfloat16)


def kernel(
    n_src, n_tgt, scale,
    x_hbm, q_hbm, y_hbm, r_hbm, g_hbm,
    gx_ref, gq_ref, gy_ref, gr_ref,
    x_in, q_in, y_in, r_in, g_in,
    a_slots, t_slots, dist_rhs, plan_rhs, t_rows, s_rows, col_acc,
    src_out, src_in, tgt_out, tgt_in,
    load_sem, a_send, a_recv, t_send, t_recv, so_send, so_recv, to_send, to_recv,
):
    f = x_in.shape[0]
    k = q_in.shape[0]
    head = f + AUG
    cols_dev = y_in.shape[1]
    me_s = lax.axis_index("src")
    me_t = lax.axis_index("tgt")

    def tgt_peer(d):
        return lax.rem(me_t + d, n_tgt)

    def src_peer(d):
        return lax.rem(me_s + d, n_src)

    loads = [
        pltpu.make_async_copy(src, dst, load_sem.at[i])
        for i, (src, dst) in enumerate(
            ((y_hbm, y_in), (r_hbm, r_in), (g_hbm, g_in), (x_hbm, x_in), (q_hbm, q_in))
        )
    ]
    for load in loads:
        load.start()

    barrier = pltpu.get_barrier_semaphore()

    def greet_tgt(d):
        pl.semaphore_signal(
            barrier, inc=1, device_id={"src": me_s, "tgt": tgt_peer(d)}, device_id_type=MESH
        )

    def greet_src(d):
        pl.semaphore_signal(
            barrier, inc=1, device_id={"src": src_peer(d), "tgt": me_t}, device_id_type=MESH
        )

    each(1, n_tgt, greet_tgt)
    each(1, n_src, greet_src)

    for load in loads:
        load.wait()

    inv_row = 1.0 / g_in[...]
    square = (k, k)
    diagonal = lax.broadcasted_iota(jnp.int32, square, 0) == lax.broadcasted_iota(
        jnp.int32, square, 1
    )
    inverse_g = jnp.sum(
        jnp.where(diagonal, jnp.broadcast_to(inv_row, square), 0.0), axis=1, keepdims=True
    )
    y = y_in[...]
    t_slots[me_s, 0:f, :] = y
    t_slots[me_s, f:head, :] = aug_rows(y, 3, 0, 1.0)
    t_slots[me_s, head:, :] = (r_in[...].astype(jnp.float32) * inverse_g).astype(jnp.bfloat16)
    x = x_in[...]
    a_slots[me_t, 0:f, :] = (x.astype(jnp.float32) * -2.0).astype(jnp.bfloat16)
    a_slots[me_t, f:head, :] = aug_rows(x, 0, 3, 0.0)
    a_slots[me_t, head:, :] = q_in[...]

    pl.semaphore_wait(barrier, n_tgt + n_src - 2)

    def t_copy(d, slot):
        return pltpu.make_async_remote_copy(
            src_ref=t_slots.at[slot], dst_ref=t_slots.at[slot],
            send_sem=t_send.at[d], recv_sem=t_recv.at[slot],
            device_id={"src": src_peer(d), "tgt": me_t}, device_id_type=MESH,
        )

    def a_copy(d, slot):
        return pltpu.make_async_remote_copy(
            src_ref=a_slots.at[slot], dst_ref=a_slots.at[slot],
            send_sem=a_send.at[d], recv_sem=a_recv.at[slot],
            device_id={"src": me_s, "tgt": tgt_peer(d)}, device_id_type=MESH,
        )

    each(1, n_src, lambda d: t_copy(d, me_s).start())
    each(1, n_tgt, lambda d: a_copy(d, me_t).start())

    each(1, n_src, lambda d: t_copy(d, src_peer(d)).wait_recv())
    for s in range(n_src):
        at = pl.ds(s * cols_dev, cols_dev)
        t_rows[:, at] = t_slots[s, 0:head, :]
        s_rows[:, at] = t_slots[s, head:, :]
        dist_rhs[0:head, at] = t_slots[s, 0:head, :]
        plan_rhs[head:, at] = t_slots[s, head:, :]
    dist_rhs[head:, :] = jnp.zeros((k, dist_rhs.shape[1]), jnp.bfloat16)
    plan_rhs[0:head, :] = jnp.zeros((head, plan_rhs.shape[1]), jnp.bfloat16)

    def so_copy(d, from_slot, to_slot):
        return pltpu.make_async_remote_copy(
            src_ref=src_out.at[from_slot], dst_ref=src_in.at[to_slot],
            send_sem=so_send.at[d], recv_sem=so_recv.at[to_slot],
            device_id={"src": me_s, "tgt": tgt_peer(d)}, device_id_type=MESH,
        )

    def block(d):
        peer = tgt_peer(d)
        static = isinstance(d, int)
        if not (static and d == 0):
            a_copy(d, peer).wait_recv()
        a = a_slots[peer]
        at = a.astype(jnp.float32).T.astype(jnp.bfloat16)
        squared = jnp.dot(at, dist_rhs[...], preferred_element_type=jnp.float32)
        plan = jnp.dot(at, plan_rhs[...], preferred_element_type=jnp.float32)
        inv = lax.rsqrt(squared)
        weight = (plan * inv).astype(jnp.bfloat16)
        cost = (squared * inv).astype(jnp.bfloat16)
        w_sum = lax.dot_general(t_rows[...], weight, NT, preferred_element_type=jnp.float32)
        c_sum = lax.dot_general(s_rows[...], cost, NT, preferred_element_type=jnp.float32)
        src_out[d, 0:f, :] = (
            a[0:f].astype(jnp.float32) * (-0.5 * w_sum[f : f + 1]) - w_sum[0:f]
        )
        src_out[d, f:, :] = c_sum
        if not (static and d == 0):
            so_copy(d, d, me_t).start()
        aw = jnp.dot(a[0:head], weight, preferred_element_type=jnp.float32)
        ac = jnp.dot(a[head:], cost, preferred_element_type=jnp.float32)
        if static and d == 0:
            col_acc[0:head, :] = aw
            col_acc[head:, :] = ac
        else:
            col_acc[0:head, :] += aw
            col_acc[head:, :] += ac

    block(0)
    each(1, n_tgt, block)

    def to_copy(d, from_slot, to_slot):
        return pltpu.make_async_remote_copy(
            src_ref=tgt_out.at[from_slot], dst_ref=tgt_in.at[to_slot],
            send_sem=to_send.at[d], recv_sem=to_recv.at[to_slot],
            device_id={"src": src_peer(d), "tgt": me_t}, device_id_type=MESH,
        )

    for s in range(n_src):
        at = pl.ds(s * cols_dev, cols_dev)
        mass = col_acc[f + 3 : f + 4, at]
        tgt_out[s, 0:f, :] = t_rows[0:f, at].astype(jnp.float32) * mass + 0.5 * col_acc[0:f, at]
        tgt_out[s, f:, :] = col_acc[head:, at]
    each(1, n_src, lambda d: to_copy(d, src_peer(d), me_s).start())

    total = [src_out[0]]

    def add_src(d):
        peer = tgt_peer(d)
        so_copy(d, d, peer).wait_recv()
        src_out[0] += src_in[peer]

    each(1, n_tgt, add_src)
    gx_ref[...] = src_out[0, 0:f, :] * scale
    gq_ref[...] = src_out[0, f:, :] * scale

    def add_tgt(d):
        peer = src_peer(d)
        to_copy(d, peer, peer).wait_recv()
        tgt_out[me_s] += tgt_in[peer]

    each(1, n_src, add_tgt)
    gy_ref[...] = tgt_out[me_s, 0:f, :] * scale
    gr_ref[...] = tgt_out[me_s, f:, :] * inverse_g * scale

    each(1, n_src, lambda d: t_copy(d, me_s).wait_send())
    each(1, n_tgt, lambda d: a_copy(d, me_t).wait_send())
    each(1, n_tgt, lambda d: so_copy(d, d, me_t).wait_send())
    each(1, n_src, lambda d: to_copy(d, src_peer(d), me_s).wait_send())


def local(src_feats, src_factor, tgt_feats, tgt_factor, rank_weight):
    n_src = lax.axis_size("src")
    n_tgt = lax.axis_size("tgt")
    f, rows = src_feats.shape
    k = src_factor.shape[0]
    cols = tgt_feats.shape[1]
    wide = n_src * cols
    stack = f + AUG + k
    f32, bf16 = jnp.float32, jnp.bfloat16
    scale = 1.0 / (cols * n_src * n_tgt)
    vmem = pl.BlockSpec(memory_space=pltpu.VMEM)
    dma = pltpu.SemaphoreType.DMA
    return pl.pallas_call(
        functools.partial(kernel, n_src, n_tgt, scale),
        out_shape=(
            jax.ShapeDtypeStruct((f, rows), f32),
            jax.ShapeDtypeStruct((k, rows), f32),
            jax.ShapeDtypeStruct((f, cols), f32),
            jax.ShapeDtypeStruct((k, cols), f32),
        ),
        in_specs=[pl.BlockSpec(memory_space=pl.ANY)] * 5,
        out_specs=(vmem,) * 4,
        scratch_shapes=[
            pltpu.VMEM((f, rows), bf16),
            pltpu.VMEM((k, rows), bf16),
            pltpu.VMEM((f, cols), bf16),
            pltpu.VMEM((k, cols), bf16),
            pltpu.VMEM((1, k), f32),
            pltpu.VMEM((n_tgt, stack, rows), bf16),
            pltpu.VMEM((n_src, stack, cols), bf16),
            pltpu.VMEM((stack, wide), bf16),
            pltpu.VMEM((stack, wide), bf16),
            pltpu.VMEM((f + AUG, wide), bf16),
            pltpu.VMEM((k, wide), bf16),
            pltpu.VMEM((stack, wide), f32),
            pltpu.VMEM((n_tgt, f + k, rows), f32),
            pltpu.VMEM((n_tgt, f + k, rows), f32),
            pltpu.VMEM((n_src, f + k, cols), f32),
            pltpu.VMEM((n_src, f + k, cols), f32),
            dma((5,)),
            dma((n_tgt,)),
            dma((n_tgt,)),
            dma((n_src,)),
            dma((n_src,)),
            dma((n_tgt,)),
            dma((n_tgt,)),
            dma((n_src,)),
            dma((n_src,)),
        ],
        compiler_params=pltpu.CompilerParams(
            collective_id=0, has_side_effects=True, vmem_limit_bytes=63 * 1024 * 1024
        ),
    )(src_feats, src_factor, tgt_feats, tgt_factor, rank_weight.reshape(1, k))


def solution(mesh):
    src = P(None, ("src", "tgt"))
    tgt = P(None, ("tgt", "src"))
    return jax.shard_map(
        local,
        mesh=mesh,
        in_specs=(src, src, tgt, tgt, P()),
        out_specs=(src, src, tgt, tgt),
        check_vma=False,
    )
```

```python
import functools

import jax
import jax.numpy as jnp
from jax import lax
from jax.experimental import pallas as pl
from jax.experimental.pallas import tpu as pltpu
from jax.sharding import PartitionSpec as P

MESH = pl.DeviceIdType.MESH
NT = (((1,), (1,)), ((), ()))
AUG = 16


def each(low, high, body):
    if high - low <= 8:
        for i in range(low, high):
            body(i)
    else:
        lax.fori_loop(low, high, lambda i, c: (body(i), c)[1], 0)


def split3(value):
    high = value.astype(jnp.bfloat16).astype(jnp.float32)
    rest = value - high
    mid = rest.astype(jnp.bfloat16).astype(jnp.float32)
    return high, mid, rest - mid


def aug_rows(feats, first, ones_at, extra):
    norm = jnp.sum(feats * feats, axis=0, keepdims=True) + extra
    high, mid, low = split3(norm)
    shape = (AUG, feats.shape[1])
    row = lax.broadcasted_iota(jnp.int32, shape, 0)
    out = jnp.where((row >= ones_at) & (row < ones_at + 3), 1.0, 0.0)
    for k, part in enumerate((high, mid, low)):
        out = jnp.where(row == first + k, jnp.broadcast_to(part, shape), out)
    return out


def kernel(
    n_src, n_tgt, low, scale,
    x_hbm, q_hbm, y_hbm, r_hbm, g_hbm,
    gx_ref, gq_ref, gy_ref, gr_ref,
    x_in, q_in, y_in, r_in, g_in,
    a_slots, t_slots, row_stack, col_stack, row_acc,
    src_out, src_in, tgt_out, tgt_in,
    load_sem, a_send, a_recv, t_send, t_recv, so_send, so_recv, to_send, to_recv,
):
    f, rows = x_in.shape
    k = q_in.shape[0]
    head = f + AUG
    stack = head + k
    half = rows // 2
    split = a_slots.shape[1]
    n_a = n_src * low
    n_b = n_tgt // low
    me_s = lax.axis_index("src")
    me_t = lax.axis_index("tgt")
    me_b = me_t // low
    me_low = me_t % low
    me_a = me_s * low + me_low

    def a_peer(d):
        return lax.rem(me_a + d, n_a)

    def b_peer(d):
        if n_b & (n_b - 1) or not isinstance(d, int):
            return lax.rem(me_b + d, n_b)
        peer, bit = me_b, 1
        while bit <= d:
            if d & bit:
                peer = peer + bit - 2 * bit * ((peer // bit) % 2)
            bit *= 2
        return peer

    def a_device(a):
        return {"src": a // low, "tgt": me_b * low + a % low}

    def b_device(b):
        return {"src": me_s, "tgt": b * low + me_low}

    loads = [
        pltpu.make_async_copy(src, dst, load_sem.at[i])
        for i, (src, dst) in enumerate(
            ((x_hbm, x_in), (q_hbm, q_in), (y_hbm, y_in), (r_hbm, r_in), (g_hbm, g_in))
        )
    ]
    for load in loads:
        load.start()

    barrier = pltpu.get_barrier_semaphore()

    def greet(device):
        pl.semaphore_signal(barrier, inc=1, device_id=device, device_id_type=MESH)

    each(1, n_a, lambda d: greet(a_device(a_peer(d))))
    each(1, n_b, lambda d: greet(b_device(b_peer(d))))

    for load in loads:
        load.wait()

    x = x_in[...].astype(jnp.float32)
    mine = jnp.concatenate([x * -2.0, aug_rows(x, 0, 3, 0.0), q_in[...].astype(jnp.float32)], 0)
    mine = mine.T.astype(jnp.bfloat16)
    a_slots[me_a, :, 0:stack] = mine[0:split]
    a_slots[me_a, 0 : rows - split, stack : 2 * stack] = mine[split:]
    inv_row = 1.0 / g_in[...]
    square = (k, k)
    diagonal = lax.broadcasted_iota(jnp.int32, square, 0) == lax.broadcasted_iota(
        jnp.int32, square, 1
    )
    inverse_g = jnp.sum(
        jnp.where(diagonal, jnp.broadcast_to(inv_row, square), 0.0), axis=1, keepdims=True
    )
    y = y_in[...]
    t_slots[me_b, 0:f, :] = y
    t_slots[me_b, f:head, :] = aug_rows(y.astype(jnp.float32), 3, 0, 1.0).astype(jnp.bfloat16)
    t_slots[me_b, head:, :] = (r_in[...].astype(jnp.float32) * inverse_g).astype(jnp.bfloat16)

    pl.semaphore_wait(barrier, n_a + n_b - 2)

    def remote(src, dst, send, recv, device):
        return pltpu.make_async_remote_copy(
            src_ref=src, dst_ref=dst, send_sem=send, recv_sem=recv,
            device_id=device, device_id_type=MESH,
        )

    def a_copy(d, slot):
        ref = a_slots.at[slot]
        return remote(ref, ref, a_send.at[d], a_recv.at[slot], a_device(a_peer(d)))

    def t_copy(d, slot):
        ref = t_slots.at[slot]
        return remote(ref, ref, t_send.at[d], t_recv.at[slot], b_device(b_peer(d)))

    def so_copy(d, slot):
        return remote(
            src_out.at[d], src_in.at[slot], so_send.at[d], so_recv.at[slot], a_device(a_peer(d))
        )

    def to_copy(d, slot):
        return remote(
            tgt_out.at[d], tgt_in.at[slot], to_send.at[d], to_recv.at[slot], b_device(b_peer(d))
        )

    each(1, n_b, lambda d: t_copy(d, me_b).start())
    each(1, n_a, lambda d: a_copy(d, me_a).start())

    each(1, n_a, lambda d: a_copy(d, a_peer(d)).wait_recv())
    for a in range(n_a):
        row_stack[a * rows : a * rows + split, :] = a_slots[a, :, 0:stack]
        row_stack[a * rows + split : (a + 1) * rows, :] = a_slots[
            a, 0 : rows - split, stack : 2 * stack
        ]
    col_stack[...] = row_stack[...].T

    def block(d):
        first = isinstance(d, int) and d == 0
        peer = b_peer(d)
        if not first:
            t_copy(d, peer).wait_recv()
        points = t_slots[peer]
        cols = points.shape[1]
        zero_low = jnp.zeros((head, cols), jnp.bfloat16)
        zero_high = jnp.zeros((k, cols), jnp.bfloat16)
        rhs = jnp.concatenate(
            [
                jnp.concatenate([points[0:head], zero_high], 0),
                jnp.concatenate([zero_low, points[head:]], 0),
            ],
            1,
        )
        both = jnp.dot(row_stack[...], rhs, preferred_element_type=jnp.float32)
        squared, plan = both[:, 0:cols], both[:, cols:]
        inv = lax.rsqrt(squared)
        terms = jnp.concatenate(
            [(plan * inv).astype(jnp.bfloat16), (squared * inv).astype(jnp.bfloat16)], 1
        )
        col = jnp.dot(col_stack[...], terms, preferred_element_type=jnp.float32)
        mass = col[f + 3 : f + 4, 0:cols]
        tgt_out[d, 0:f, :] = points[0:f].astype(jnp.float32) * mass + 0.5 * col[0:f, 0:cols]
        tgt_out[d, f:, :] = col[head:, cols:]
        if not first:
            to_copy(d, me_b).start()
        row = lax.dot_general(terms, rhs, NT, preferred_element_type=jnp.float32)
        if first:
            row_acc[...] = row
        else:
            row_acc[...] += row

    block(0)
    each(1, n_b, block)

    def pack(d):
        start = pl.multiple_of(a_peer(d) * rows, 8)
        src_out[d, :, 0:stack] = row_acc[pl.ds(start, half), :]
        src_out[d, :, stack : 2 * stack] = row_acc[pl.ds(start + half, half), :]
        so_copy(d, me_a).start()

    each(1, n_a, pack)
    mine = pl.multiple_of(me_a * rows, 8)
    src_out[0, :, 0:stack] = row_acc[pl.ds(mine, half), :]
    src_out[0, :, stack : 2 * stack] = row_acc[pl.ds(mine + half, half), :]

    def add_tgt(d):
        peer = b_peer(d)
        to_copy(d, peer).wait_recv()
        tgt_out[0] += tgt_in[peer]

    each(1, n_b, add_tgt)
    gy_ref[...] = tgt_out[0, 0:f, :] * scale
    gr_ref[...] = tgt_out[0, f:, :] * inverse_g * scale

    def add_src(d):
        peer = a_peer(d)
        so_copy(d, peer).wait_recv()
        src_out[0] += src_in[peer]

    each(1, n_a, add_src)
    total = src_out[0]
    total = jnp.concatenate([total[:, 0:stack], total[:, stack : 2 * stack]], 0).T
    gx_ref[...] = (x * total[f : f + 1] - total[0:f]) * scale
    gq_ref[...] = total[head:] * scale

    each(1, n_a, lambda d: a_copy(d, me_a).wait_send())
    each(1, n_b, lambda d: t_copy(d, me_b).wait_send())
    each(1, n_a, lambda d: so_copy(d, me_a).wait_send())
    each(1, n_b, lambda d: to_copy(d, me_b).wait_send())


def place(*refs):
    sources, places, sems = refs[0:4], refs[4:8], refs[8]
    copies = [
        pltpu.make_async_copy(src, dst, sems.at[i])
        for i, (src, dst) in enumerate(zip(sources, places))
    ]
    for copy in copies:
        copy.start()
    for copy in copies:
        copy.wait()


def local(src_feats, src_factor, tgt_feats, tgt_factor, rank_weight):
    n_src = lax.axis_size("src")
    n_tgt = lax.axis_size("tgt")
    low = 2 if n_tgt % 2 == 0 else 1
    n_a, n_b = n_src * low, n_tgt // low
    f, rows = src_feats.shape
    k = src_factor.shape[0]
    cols = tgt_feats.shape[1]
    stack = f + AUG + k
    split = (rows // 2 + 15) // 16 * 16
    f32, bf16 = jnp.float32, jnp.bfloat16
    scale = 1.0 / (cols * n_src * n_tgt)
    vmem = pl.BlockSpec(memory_space=pltpu.VMEM)
    hbm = pl.BlockSpec(memory_space=pltpu.HBM)
    anywhere = pl.BlockSpec(memory_space=pl.ANY)
    dma = pltpu.SemaphoreType.DMA
    out_shape = (
        jax.ShapeDtypeStruct((f, rows), f32),
        jax.ShapeDtypeStruct((k, rows), f32),
        jax.ShapeDtypeStruct((f, cols), f32),
        jax.ShapeDtypeStruct((k, cols), f32),
    )
    results = pl.pallas_call(
        functools.partial(kernel, n_src, n_tgt, low, scale),
        out_shape=tuple(pltpu.VMEM(o.shape, o.dtype) for o in out_shape),
        in_specs=[hbm] * 5,
        out_specs=(vmem,) * 4,
        scratch_shapes=[
            pltpu.VMEM((f, rows), bf16),
            pltpu.VMEM((k, rows), bf16),
            pltpu.VMEM((f, cols), bf16),
            pltpu.VMEM((k, cols), bf16),
            pltpu.VMEM((1, k), f32),
            pltpu.VMEM((n_a, split, 2 * stack), bf16),
            pltpu.VMEM((n_b, stack, cols), bf16),
            pltpu.VMEM((n_a * rows, stack), bf16),
            pltpu.VMEM((stack, n_a * rows), bf16),
            pltpu.VMEM((n_a * rows, stack), f32),
            pltpu.VMEM((n_a, rows // 2, 2 * stack), f32),
            pltpu.VMEM((n_a, rows // 2, 2 * stack), f32),
            pltpu.VMEM((n_b, f + k, cols), f32),
            pltpu.VMEM((n_b, f + k, cols), f32),
            dma((5,)),
            dma((n_a,)),
            dma((n_a,)),
            dma((n_b,)),
            dma((n_b,)),
            dma((n_a,)),
            dma((n_a,)),
            dma((n_b,)),
            dma((n_b,)),
        ],
        compiler_params=pltpu.CompilerParams(
            collective_id=0, has_side_effects=True, vmem_limit_bytes=63 * 1024 * 1024
        ),
    )(src_feats, src_factor, tgt_feats, tgt_factor, rank_weight.reshape(1, k))
    return pl.pallas_call(
        place,
        out_shape=out_shape,
        in_specs=[anywhere] * 4,
        out_specs=(hbm,) * 4,
        scratch_shapes=[dma((4,))],
    )(*results)


def solution(mesh):
    src = P(None, ("src", "tgt"))
    tgt = P(None, ("tgt", "src"))
    return jax.shard_map(
        local,
        mesh=mesh,
        in_specs=(src, src, tgt, tgt, P()),
        out_specs=(src, src, tgt, tgt),
        check_vma=False,
    )
```

```python
import functools

import jax
import jax.numpy as jnp
from jax import lax
from jax.experimental import pallas as pl
from jax.experimental.pallas import tpu as pltpu
from jax.sharding import PartitionSpec as P

MESH = pl.DeviceIdType.MESH
NT = (((1,), (1,)), ((), ()))
AUG = 16


def each(low, high, body):
    if high - low <= 8:
        for i in range(low, high):
            body(i)
    else:
        lax.fori_loop(low, high, lambda i, c: (body(i), c)[1], 0)


def fold(low, high, start, body):
    if high - low <= 8:
        for i in range(low, high):
            start = body(i, start)
        return start
    return lax.fori_loop(low, high, body, start)


def split3(value):
    high = value.astype(jnp.bfloat16).astype(jnp.float32)
    rest = value - high
    mid = rest.astype(jnp.bfloat16).astype(jnp.float32)
    return high, mid, rest - mid


def aug_rows(feats, first, ones_at, extra):
    norm = jnp.sum(feats * feats, axis=0, keepdims=True) + extra
    high, mid, low = split3(norm)
    shape = (AUG, feats.shape[1])
    row = lax.broadcasted_iota(jnp.int32, shape, 0)
    out = jnp.where((row >= ones_at) & (row < ones_at + 3), 1.0, 0.0)
    for k, part in enumerate((high, mid, low)):
        out = jnp.where(row == first + k, jnp.broadcast_to(part, shape), out)
    return out


def kernel(
    n_src, n_tgt, low, scale,
    x_hbm, q_hbm, y_hbm, r_hbm, g_hbm,
    gx_ref, gq_ref, gy_ref, gr_ref,
    x_in, q_in, y_in, r_in, g_in,
    a_slots, t_slots, row_stack, col_stack, row_acc,
    src_out, src_in, tgt_out, tgt_in,
    load_sem, a_send, a_recv, t_send, t_recv, so_send, so_recv, to_send, to_recv,
):
    f, rows = x_in.shape
    k = q_in.shape[0]
    head = f + AUG
    stack = head + k
    half = rows // 2
    split = a_slots.shape[1]
    n_a = n_src * low
    n_b = n_tgt // low
    me_s = lax.axis_index("src")
    me_t = lax.axis_index("tgt")
    me_b = me_t // low
    me_low = me_t % low
    me_a = me_s * low + me_low

    def a_peer(d):
        return lax.rem(me_a + d, n_a)

    def b_peer(d):
        if n_b & (n_b - 1) or not isinstance(d, int):
            return lax.rem(me_b + d, n_b)
        peer, bit = me_b, 1
        while bit <= d:
            if d & bit:
                peer = peer + bit - 2 * bit * ((peer // bit) % 2)
            bit *= 2
        return peer

    def a_device(a):
        return {"src": a // low, "tgt": me_b * low + a % low}

    def b_device(b):
        return {"src": me_s, "tgt": b * low + me_low}

    loads = [
        pltpu.make_async_copy(src, dst, load_sem.at[i])
        for i, (src, dst) in enumerate(
            ((x_hbm, x_in), (q_hbm, q_in), (y_hbm, y_in), (r_hbm, r_in), (g_hbm, g_in))
        )
    ]
    for load in loads:
        load.start()

    barrier = pltpu.get_barrier_semaphore()

    def greet(device):
        pl.semaphore_signal(barrier, inc=1, device_id=device, device_id_type=MESH)

    each(1, n_a, lambda d: greet(a_device(a_peer(d))))
    each(1, n_b, lambda d: greet(b_device(b_peer(d))))

    for load in loads:
        load.wait()

    x = x_in[...].astype(jnp.float32)
    mine = jnp.concatenate([x * -2.0, aug_rows(x, 0, 3, 0.0), q_in[...].astype(jnp.float32)], 0)
    mine = mine.T.astype(jnp.bfloat16)
    a_slots[me_a, :, 0:stack] = mine[0:split]
    a_slots[me_a, 0 : rows - split, stack : 2 * stack] = mine[split:]
    inv_row = 1.0 / g_in[...]
    square = (k, k)
    diagonal = lax.broadcasted_iota(jnp.int32, square, 0) == lax.broadcasted_iota(
        jnp.int32, square, 1
    )
    inverse_g = jnp.sum(
        jnp.where(diagonal, jnp.broadcast_to(inv_row, square), 0.0), axis=1, keepdims=True
    )
    y = y_in[...]
    t_slots[me_b, 0:f, :] = y
    t_slots[me_b, f:head, :] = aug_rows(y.astype(jnp.float32), 3, 0, 1.0).astype(jnp.bfloat16)
    t_slots[me_b, head:, :] = (r_in[...].astype(jnp.float32) * inverse_g).astype(jnp.bfloat16)

    pl.semaphore_wait(barrier, n_a + n_b - 2)

    def remote(src, dst, send, recv, device):
        return pltpu.make_async_remote_copy(
            src_ref=src, dst_ref=dst, send_sem=send, recv_sem=recv,
            device_id=device, device_id_type=MESH,
        )

    def wait_all(slots, sem):
        ref = slots.at[pl.ds(0, slots.shape[0] - 1)]
        pltpu.make_async_copy(ref, ref, sem.at[0]).wait()

    def a_copy(d, slot):
        ref = a_slots.at[slot]
        return remote(ref, ref, a_send.at[0], a_recv.at[0], a_device(a_peer(d)))

    def t_copy(d, slot):
        ref = t_slots.at[slot]
        return remote(ref, ref, t_send.at[0], t_recv.at[slot], b_device(b_peer(d)))

    def so_copy(d, slot):
        return remote(
            src_out.at[d], src_in.at[slot], so_send.at[0], so_recv.at[0], a_device(a_peer(d))
        )

    def to_copy(d, slot):
        return remote(
            tgt_out.at[d], tgt_in.at[slot], to_send.at[0], to_recv.at[0], b_device(b_peer(d))
        )

    each(1, n_b, lambda d: t_copy(d, me_b).start())
    each(1, n_a, lambda d: a_copy(d, me_a).start())

    wait_all(a_slots, a_recv)
    for a in range(n_a):
        row_stack[a * rows : a * rows + split, :] = a_slots[a, :, 0:stack]
        row_stack[a * rows + split : (a + 1) * rows, :] = a_slots[
            a, 0 : rows - split, stack : 2 * stack
        ]
    col_stack[...] = row_stack[...].T

    def block(d):
        first = isinstance(d, int) and d == 0
        peer = b_peer(d)
        if not first:
            t_copy(d, peer).wait_recv()
        points = t_slots[peer]
        cols = points.shape[1]
        zero_low = jnp.zeros((head, cols), jnp.bfloat16)
        zero_high = jnp.zeros((k, cols), jnp.bfloat16)
        rhs = jnp.concatenate(
            [
                jnp.concatenate([points[0:head], zero_high], 0),
                jnp.concatenate([zero_low, points[head:]], 0),
            ],
            1,
        )
        both = jnp.dot(row_stack[...], rhs, preferred_element_type=jnp.float32)
        squared, plan = both[:, 0:cols], both[:, cols:]
        inv = lax.rsqrt(squared)
        terms = jnp.concatenate(
            [(plan * inv).astype(jnp.bfloat16), (squared * inv).astype(jnp.bfloat16)], 1
        )
        col = jnp.dot(col_stack[...], terms, preferred_element_type=jnp.float32)
        mass = col[f + 3 : f + 4, 0:cols]
        tgt_out[d, 0:f, :] = points[0:f].astype(jnp.float32) * mass + 0.5 * col[0:f, 0:cols]
        tgt_out[d, f:, :] = col[head:, cols:]
        if not first:
            to_copy(d, me_b).start()
        row = lax.dot_general(terms, rhs, NT, preferred_element_type=jnp.float32)
        if first:
            row_acc[...] = row
        else:
            row_acc[...] += row

    block(0)
    each(1, n_b, block)

    def pack(d):
        start = pl.multiple_of(a_peer(d) * rows, 8)
        src_out[d, :, 0:stack] = row_acc[pl.ds(start, half), :]
        src_out[d, :, stack : 2 * stack] = row_acc[pl.ds(start + half, half), :]
        so_copy(d, me_a).start()

    each(1, n_a, pack)
    mine = pl.multiple_of(me_a * rows, 8)
    src_out[0, :, 0:stack] = row_acc[pl.ds(mine, half), :]
    src_out[0, :, stack : 2 * stack] = row_acc[pl.ds(mine + half, half), :]

    wait_all(tgt_in, to_recv)
    total = fold(1, n_b, tgt_out[0], lambda d, sum_: sum_ + tgt_in[b_peer(d)])
    gy_ref[...] = total[0:f] * scale
    gr_ref[...] = total[f:] * inverse_g * scale

    wait_all(src_in, so_recv)
    total = fold(1, n_a, src_out[0], lambda d, sum_: sum_ + src_in[a_peer(d)])
    total = jnp.concatenate([total[:, 0:stack], total[:, stack : 2 * stack]], 0).T
    gx_ref[...] = (x * total[f : f + 1] - total[0:f]) * scale
    gq_ref[...] = total[head:] * scale

    wait_all(a_slots, a_send)
    wait_all(t_slots, t_send)
    wait_all(src_out, so_send)
    wait_all(tgt_out, to_send)


def place(*refs):
    sources, places, sems = refs[0:4], refs[4:8], refs[8]
    copies = [
        pltpu.make_async_copy(src, dst, sems.at[i])
        for i, (src, dst) in enumerate(zip(sources, places))
    ]
    for copy in copies:
        copy.start()
    for copy in copies:
        copy.wait()


def local(src_feats, src_factor, tgt_feats, tgt_factor, rank_weight):
    n_src = lax.axis_size("src")
    n_tgt = lax.axis_size("tgt")
    low = 2 if n_tgt % 2 == 0 else 1
    n_a, n_b = n_src * low, n_tgt // low
    f, rows = src_feats.shape
    k = src_factor.shape[0]
    cols = tgt_feats.shape[1]
    stack = f + AUG + k
    split = (rows // 2 + 15) // 16 * 16
    f32, bf16 = jnp.float32, jnp.bfloat16
    scale = 1.0 / (cols * n_src * n_tgt)
    vmem = pl.BlockSpec(memory_space=pltpu.VMEM)
    hbm = pl.BlockSpec(memory_space=pltpu.HBM)
    dma = pltpu.SemaphoreType.DMA
    out_shape = (
        jax.ShapeDtypeStruct((f, rows), f32),
        jax.ShapeDtypeStruct((k, rows), f32),
        jax.ShapeDtypeStruct((f, cols), f32),
        jax.ShapeDtypeStruct((k, cols), f32),
    )
    results = pl.pallas_call(
        functools.partial(kernel, n_src, n_tgt, low, scale),
        out_shape=tuple(pltpu.VMEM(o.shape, o.dtype) for o in out_shape),
        in_specs=[hbm] * 5,
        out_specs=(vmem,) * 4,
        scratch_shapes=[
            pltpu.VMEM((f, rows), bf16),
            pltpu.VMEM((k, rows), bf16),
            pltpu.VMEM((f, cols), bf16),
            pltpu.VMEM((k, cols), bf16),
            pltpu.VMEM((1, k), f32),
            pltpu.VMEM((n_a, split, 2 * stack), bf16),
            pltpu.VMEM((n_b, stack, cols), bf16),
            pltpu.VMEM((n_a * rows, stack), bf16),
            pltpu.VMEM((stack, n_a * rows), bf16),
            pltpu.VMEM((n_a * rows, stack), f32),
            pltpu.VMEM((n_a, rows // 2, 2 * stack), f32),
            pltpu.VMEM((n_a, rows // 2, 2 * stack), f32),
            pltpu.VMEM((n_b, f + k, cols), f32),
            pltpu.VMEM((n_b, f + k, cols), f32),
            dma((5,)),
            dma((n_a,)),
            dma((n_a,)),
            dma((n_b,)),
            dma((n_b,)),
            dma((n_a,)),
            dma((n_a,)),
            dma((n_b,)),
            dma((n_b,)),
        ],
        compiler_params=pltpu.CompilerParams(
            collective_id=0, has_side_effects=True, vmem_limit_bytes=63 * 1024 * 1024
        ),
    )(src_feats, src_factor, tgt_feats, tgt_factor, rank_weight.reshape(1, k))
    return pl.pallas_call(
        place,
        out_shape=out_shape,
        in_specs=[vmem] * 4,
        out_specs=(hbm,) * 4,
        scratch_shapes=[dma((4,))],
    )(*(pltpu.with_memory_space_constraint(r, pltpu.VMEM) for r in results))


def solution(mesh):
    src = P(None, ("src", "tgt"))
    tgt = P(None, ("tgt", "src"))
    return jax.shard_map(
        local,
        mesh=mesh,
        in_specs=(src, src, tgt, tgt, P()),
        out_specs=(src, src, tgt, tgt),
        check_vma=False,
    )
```

```python
import functools

import jax
import jax.numpy as jnp
from jax import lax
from jax.experimental import pallas as pl
from jax.experimental.pallas import tpu as pltpu
from jax.sharding import PartitionSpec as P

MESH = pl.DeviceIdType.MESH
NT = (((1,), (1,)), ((), ()))
AUG = 16
CHUNK = 128


def each(low, high, body):
    if high - low <= 8:
        for i in range(low, high):
            body(i)
    else:
        lax.fori_loop(low, high, lambda i, c: (body(i), c)[1], 0)


def fold(low, high, start, body):
    if high - low <= 8:
        for i in range(low, high):
            start = body(i, start)
        return start
    return lax.fori_loop(low, high, body, start)


def split3(value):
    high = value.astype(jnp.bfloat16).astype(jnp.float32)
    rest = value - high
    mid = rest.astype(jnp.bfloat16).astype(jnp.float32)
    return high, mid, rest - mid


def aug_rows(feats, first, ones_at, extra):
    norm = jnp.sum(feats * feats, axis=0, keepdims=True) + extra
    high, mid, low = split3(norm)
    shape = (AUG, feats.shape[1])
    row = lax.broadcasted_iota(jnp.int32, shape, 0)
    out = jnp.where((row >= ones_at) & (row < ones_at + 3), 1.0, 0.0)
    for k, part in enumerate((high, mid, low)):
        out = jnp.where(row == first + k, jnp.broadcast_to(part, shape), out)
    return out


def kernel(
    n_src, n_tgt, low, scale,
    x_hbm, q_hbm, y_hbm, r_hbm, g_hbm,
    gx_ref, gq_ref, gy_ref, gr_ref,
    x_in, q_in, y_in, r_in, g_in,
    a_slots, t_slots, row_stack, col_stack, row_acc,
    src_out, src_in, tgt_out, tgt_in,
    load_sem, a_send, a_recv, t_send, t_recv, so_send, so_recv, to_send, to_recv,
):
    f, rows = x_in.shape
    k = q_in.shape[0]
    head = f + AUG
    stack = head + k
    half = rows // 2
    split = a_slots.shape[1]
    n_a = n_src * low
    n_b = n_tgt // low
    me_s = lax.axis_index("src")
    me_t = lax.axis_index("tgt")
    me_b = me_t // low
    me_low = me_t % low
    me_a = me_s * low + me_low

    def a_peer(d):
        return lax.rem(me_a + d, n_a)

    def b_peer(d):
        if n_b & (n_b - 1) or not isinstance(d, int):
            return lax.rem(me_b + d, n_b)
        peer, bit = me_b, 1
        while bit <= d:
            if d & bit:
                peer = peer + bit - 2 * bit * ((peer // bit) % 2)
            bit *= 2
        return peer

    def a_device(a):
        return {"src": a // low, "tgt": me_b * low + a % low}

    def b_device(b):
        return {"src": me_s, "tgt": b * low + me_low}

    loads = [
        pltpu.make_async_copy(src, dst, load_sem.at[i])
        for i, (src, dst) in enumerate(
            ((x_hbm, x_in), (q_hbm, q_in), (y_hbm, y_in), (r_hbm, r_in), (g_hbm, g_in))
        )
    ]
    for load in loads:
        load.start()

    barrier = pltpu.get_barrier_semaphore()

    def greet(device):
        pl.semaphore_signal(barrier, inc=1, device_id=device, device_id_type=MESH)

    each(1, n_a, lambda d: greet(a_device(a_peer(d))))
    each(1, n_b, lambda d: greet(b_device(b_peer(d))))

    for load in loads:
        load.wait()

    x = x_in[...].astype(jnp.float32)
    mine = jnp.concatenate([x * -2.0, aug_rows(x, 0, 3, 0.0), q_in[...].astype(jnp.float32)], 0)
    mine = mine.T.astype(jnp.bfloat16)
    a_slots[me_a, :, 0:stack] = mine[0:split]
    a_slots[me_a, 0 : rows - split, stack : 2 * stack] = mine[split:]
    inv_row = 1.0 / g_in[...]
    square = (k, k)
    diagonal = lax.broadcasted_iota(jnp.int32, square, 0) == lax.broadcasted_iota(
        jnp.int32, square, 1
    )
    inverse_g = jnp.sum(
        jnp.where(diagonal, jnp.broadcast_to(inv_row, square), 0.0), axis=1, keepdims=True
    )
    y = y_in[...]
    t_slots[me_b, 0:f, :] = y
    t_slots[me_b, f:head, :] = aug_rows(y.astype(jnp.float32), 3, 0, 1.0).astype(jnp.bfloat16)
    t_slots[me_b, head:, :] = (r_in[...].astype(jnp.float32) * inverse_g).astype(jnp.bfloat16)

    pl.semaphore_wait(barrier, n_a + n_b - 2)

    def remote(src, dst, send, recv, device):
        return pltpu.make_async_remote_copy(
            src_ref=src, dst_ref=dst, send_sem=send, recv_sem=recv,
            device_id=device, device_id_type=MESH,
        )

    def wait_all(slots, sem):
        ref = slots.at[pl.ds(0, slots.shape[0] - 1)]
        pltpu.make_async_copy(ref, ref, sem.at[0]).wait()

    def a_copy(d, slot):
        ref = a_slots.at[slot]
        return remote(ref, ref, a_send.at[0], a_recv.at[0], a_device(a_peer(d)))

    def t_copy(d, slot):
        ref = t_slots.at[slot]
        return remote(ref, ref, t_send.at[0], t_recv.at[slot], b_device(b_peer(d)))

    def so_copy(d, slot):
        return remote(
            src_out.at[d], src_in.at[slot], so_send.at[0], so_recv.at[0], a_device(a_peer(d))
        )

    def to_copy(d, slot):
        return remote(
            tgt_out.at[d], tgt_in.at[slot], to_send.at[0], to_recv.at[0], b_device(b_peer(d))
        )

    each(1, n_a, lambda d: a_copy(d, me_a).start())
    each(1, n_b, lambda d: t_copy(d, me_b).start())

    wait_all(a_slots, a_recv)
    for a in range(n_a):
        row_stack[a * rows : a * rows + split, :] = a_slots[a, :, 0:stack]
        row_stack[a * rows + split : (a + 1) * rows, :] = a_slots[
            a, 0 : rows - split, stack : 2 * stack
        ]
    col_stack[...] = row_stack[...].T

    def block(d):
        first = isinstance(d, int) and d == 0
        peer = b_peer(d)
        if not first:
            t_copy(d, peer).wait_recv()
        points = t_slots[peer]
        cols = points.shape[1]
        zero_low = jnp.zeros((head, cols), jnp.bfloat16)
        zero_high = jnp.zeros((k, cols), jnp.bfloat16)
        rhs = jnp.concatenate(
            [
                jnp.concatenate([points[0:head], zero_high], 0),
                jnp.concatenate([zero_low, points[head:]], 0),
            ],
            1,
        )

        def chunk(start, size, col):
            part = row_stack[pl.ds(start, size), :]
            both = jnp.dot(part, rhs, preferred_element_type=jnp.float32)
            squared, plan = both[:, 0:cols], both[:, cols:]
            inv = lax.rsqrt(squared)
            terms = jnp.concatenate(
                [(plan * inv).astype(jnp.bfloat16), (squared * inv).astype(jnp.bfloat16)], 1
            )
            row = lax.dot_general(terms, rhs, NT, preferred_element_type=jnp.float32)
            if first:
                row_acc[pl.ds(start, size), :] = row
            else:
                row_acc[pl.ds(start, size), :] += row
            return col + jnp.dot(
                col_stack[:, pl.ds(start, size)], terms, preferred_element_type=jnp.float32
            )

        col = jnp.zeros((stack, 2 * cols), jnp.float32)
        total_rows = row_stack.shape[0]
        count = total_rows // CHUNK
        if count <= 8:
            for c in range(count):
                col = chunk(c * CHUNK, CHUNK, col)
        else:
            col = lax.fori_loop(
                0, count, lambda c, v: chunk(pl.multiple_of(c * CHUNK, CHUNK), CHUNK, v), col
            )
        if total_rows % CHUNK:
            col = chunk(count * CHUNK, total_rows % CHUNK, col)
        mass = col[f + 3 : f + 4, 0:cols]
        tgt_out[d, 0:f, :] = points[0:f].astype(jnp.float32) * mass + 0.5 * col[0:f, 0:cols]
        tgt_out[d, f:, :] = col[head:, cols:]
        if not first:
            to_copy(d, me_b).start()

    block(0)
    each(1, n_b, block)

    def pack(d):
        start = pl.multiple_of(a_peer(d) * rows, 8)
        src_out[d, :, 0:stack] = row_acc[pl.ds(start, half), :]
        src_out[d, :, stack : 2 * stack] = row_acc[pl.ds(start + half, half), :]
        so_copy(d, me_a).start()

    each(1, n_a, pack)
    mine = pl.multiple_of(me_a * rows, 8)
    src_out[0, :, 0:stack] = row_acc[pl.ds(mine, half), :]
    src_out[0, :, stack : 2 * stack] = row_acc[pl.ds(mine + half, half), :]

    wait_all(tgt_in, to_recv)
    total = fold(1, n_b, tgt_out[0], lambda d, sum_: sum_ + tgt_in[b_peer(d)])
    gy_ref[...] = total[0:f] * scale
    gr_ref[...] = total[f:] * inverse_g * scale

    wait_all(src_in, so_recv)
    total = fold(1, n_a, src_out[0], lambda d, sum_: sum_ + src_in[a_peer(d)])
    total = jnp.concatenate([total[:, 0:stack], total[:, stack : 2 * stack]], 0).T
    gx_ref[...] = (x * total[f : f + 1] - total[0:f]) * scale
    gq_ref[...] = total[head:] * scale

    wait_all(a_slots, a_send)
    wait_all(t_slots, t_send)
    wait_all(src_out, so_send)
    wait_all(tgt_out, to_send)


def place(*refs):
    sources, places, sems = refs[0:4], refs[4:8], refs[8]
    copies = [
        pltpu.make_async_copy(src, dst, sems.at[i])
        for i, (src, dst) in enumerate(zip(sources, places))
    ]
    for copy in copies:
        copy.start()
    for copy in copies:
        copy.wait()


def local(src_feats, src_factor, tgt_feats, tgt_factor, rank_weight):
    n_src = lax.axis_size("src")
    n_tgt = lax.axis_size("tgt")
    low = 2 if n_tgt % 2 == 0 else 1
    n_a, n_b = n_src * low, n_tgt // low
    f, rows = src_feats.shape
    k = src_factor.shape[0]
    cols = tgt_feats.shape[1]
    stack = f + AUG + k
    split = (rows // 2 + 15) // 16 * 16
    f32, bf16 = jnp.float32, jnp.bfloat16
    scale = 1.0 / (cols * n_src * n_tgt)
    vmem = pl.BlockSpec(memory_space=pltpu.VMEM)
    hbm = pl.BlockSpec(memory_space=pltpu.HBM)
    dma = pltpu.SemaphoreType.DMA
    out_shape = (
        jax.ShapeDtypeStruct((f, rows), f32),
        jax.ShapeDtypeStruct((k, rows), f32),
        jax.ShapeDtypeStruct((f, cols), f32),
        jax.ShapeDtypeStruct((k, cols), f32),
    )
    results = pl.pallas_call(
        functools.partial(kernel, n_src, n_tgt, low, scale),
        out_shape=tuple(pltpu.VMEM(o.shape, o.dtype) for o in out_shape),
        in_specs=[hbm] * 5,
        out_specs=(vmem,) * 4,
        scratch_shapes=[
            pltpu.VMEM((f, rows), bf16),
            pltpu.VMEM((k, rows), bf16),
            pltpu.VMEM((f, cols), bf16),
            pltpu.VMEM((k, cols), bf16),
            pltpu.VMEM((1, k), f32),
            pltpu.VMEM((n_a, split, 2 * stack), bf16),
            pltpu.VMEM((n_b, stack, cols), bf16),
            pltpu.VMEM((n_a * rows, stack), bf16),
            pltpu.VMEM((stack, n_a * rows), bf16),
            pltpu.VMEM((n_a * rows, stack), f32),
            pltpu.VMEM((n_a, rows // 2, 2 * stack), f32),
            pltpu.VMEM((n_a, rows // 2, 2 * stack), f32),
            pltpu.VMEM((n_b, f + k, cols), f32),
            pltpu.VMEM((n_b, f + k, cols), f32),
            dma((5,)),
            dma((n_a,)),
            dma((n_a,)),
            dma((n_b,)),
            dma((n_b,)),
            dma((n_a,)),
            dma((n_a,)),
            dma((n_b,)),
            dma((n_b,)),
        ],
        compiler_params=pltpu.CompilerParams(
            collective_id=0, has_side_effects=True, vmem_limit_bytes=63 * 1024 * 1024
        ),
    )(src_feats, src_factor, tgt_feats, tgt_factor, rank_weight.reshape(1, k))
    return pl.pallas_call(
        place,
        out_shape=out_shape,
        in_specs=[vmem] * 4,
        out_specs=(hbm,) * 4,
        scratch_shapes=[dma((4,))],
    )(*(pltpu.with_memory_space_constraint(r, pltpu.VMEM) for r in results))


def solution(mesh):
    src = P(None, ("src", "tgt"))
    tgt = P(None, ("tgt", "src"))
    return jax.shard_map(
        local,
        mesh=mesh,
        in_specs=(src, src, tgt, tgt, P()),
        out_specs=(src, src, tgt, tgt),
        check_vma=False,
    )
```

```python
import functools

import jax
import jax.numpy as jnp
from jax import lax
from jax.experimental import pallas as pl
from jax.experimental.pallas import tpu as pltpu
from jax.sharding import PartitionSpec as P

MESH = pl.DeviceIdType.MESH
NT = (((1,), (1,)), ((), ()))
AUG = 16


def each(low, high, body):
    if high - low <= 8:
        for i in range(low, high):
            body(i)
    else:
        lax.fori_loop(low, high, lambda i, c: (body(i), c)[1], 0)


def fold(low, high, start, body):
    if high - low <= 8:
        for i in range(low, high):
            start = body(i, start)
        return start
    return lax.fori_loop(low, high, body, start)


def split3(value):
    high = value.astype(jnp.bfloat16).astype(jnp.float32)
    rest = value - high
    mid = rest.astype(jnp.bfloat16).astype(jnp.float32)
    return high, mid, rest - mid


def aug_rows(feats, first, ones_at, extra):
    norm = jnp.sum(feats * feats, axis=0, keepdims=True) + extra
    high, mid, low = split3(norm)
    shape = (AUG, feats.shape[1])
    row = lax.broadcasted_iota(jnp.int32, shape, 0)
    out = jnp.where((row >= ones_at) & (row < ones_at + 3), 1.0, 0.0)
    for k, part in enumerate((high, mid, low)):
        out = jnp.where(row == first + k, jnp.broadcast_to(part, shape), out)
    return out


def kernel(
    n_src, n_tgt, low, scale,
    x_hbm, q_hbm, y_hbm, r_hbm, g_hbm,
    gx_ref, gq_ref, gy_ref, gr_ref,
    x_in, q_in, y_in, r_in, g_in,
    a_slots, t_slots, row_stack, col_stack, row_acc,
    src_out, src_in, tgt_out, tgt_in,
    load_sem, a_send, a_recv, t_send, t_recv, so_send, so_recv, to_send, to_recv,
):
    f, rows = x_in.shape
    k = q_in.shape[0]
    head = f + AUG
    stack = head + k
    half = rows // 2
    split = a_slots.shape[1]
    n_a = n_src * low
    n_b = n_tgt // low
    me_s = lax.axis_index("src")
    me_t = lax.axis_index("tgt")
    me_b = me_t // low
    me_low = me_t % low
    me_a = me_s * low + me_low

    def a_peer(d):
        return lax.rem(me_a + d, n_a)

    def b_peer(d):
        return lax.rem(me_b + d, n_b)

    def when(condition, body):
        pl.when(condition)(body)

    def a_device(a):
        return {"src": a // low, "tgt": me_b * low + a % low}

    def b_device(b):
        return {"src": me_s, "tgt": b * low + me_low}

    loads = [
        pltpu.make_async_copy(src, dst, load_sem.at[i])
        for i, (src, dst) in enumerate(
            ((x_hbm, x_in), (q_hbm, q_in), (y_hbm, y_in), (r_hbm, r_in), (g_hbm, g_in))
        )
    ]
    for load in loads:
        load.start()

    barrier = pltpu.get_barrier_semaphore()

    def greet(device):
        pl.semaphore_signal(barrier, inc=1, device_id=device, device_id_type=MESH)

    each(1, n_a, lambda d: greet(a_device(a_peer(d))))
    top = n_b - 1
    each(0, n_b, lambda j: when((j > me_b) | (j == me_b - 1), lambda: greet(b_device(j))))

    for load in loads:
        load.wait()

    x = x_in[...].astype(jnp.float32)
    mine = jnp.concatenate([x * -2.0, aug_rows(x, 0, 3, 0.0), q_in[...].astype(jnp.float32)], 0)
    mine = mine.T.astype(jnp.bfloat16)
    a_slots[me_a, :, 0:stack] = mine[0:split]
    a_slots[me_a, 0 : rows - split, stack : 2 * stack] = mine[split:]
    inv_row = 1.0 / g_in[...]
    square = (k, k)
    diagonal = lax.broadcasted_iota(jnp.int32, square, 0) == lax.broadcasted_iota(
        jnp.int32, square, 1
    )
    inverse_g = jnp.sum(
        jnp.where(diagonal, jnp.broadcast_to(inv_row, square), 0.0), axis=1, keepdims=True
    )
    y = y_in[...]
    t_slots[me_b, 0:f, :] = y
    t_slots[me_b, f:head, :] = aug_rows(y.astype(jnp.float32), 3, 0, 1.0).astype(jnp.bfloat16)
    t_slots[me_b, head:, :] = (r_in[...].astype(jnp.float32) * inverse_g).astype(jnp.bfloat16)

    pl.semaphore_wait(barrier, n_a - 1 + me_b + jnp.where(me_b < top, 1, 0))

    def remote(src, dst, send, recv, device):
        return pltpu.make_async_remote_copy(
            src_ref=src, dst_ref=dst, send_sem=send, recv_sem=recv,
            device_id=device, device_id_type=MESH,
        )

    def wait_all(slots, sem):
        ref = slots.at[pl.ds(0, slots.shape[0] - 1)]
        pltpu.make_async_copy(ref, ref, sem.at[0]).wait()

    def a_copy(d, slot):
        ref = a_slots.at[slot]
        return remote(ref, ref, a_send.at[0], a_recv.at[0], a_device(a_peer(d)))

    def t_copy(to, slot, sem):
        ref = t_slots.at[slot]
        return remote(ref, ref, sem, t_recv.at[slot], b_device(to))

    def t_down(j):
        return t_copy(j, me_b, t_send.at[0, j])

    def t_up(j):
        return t_copy(me_b + 1, j, t_send.at[1, j])

    def so_copy(d, slot):
        return remote(
            src_out.at[d], src_in.at[slot], so_send.at[0], so_recv.at[0], a_device(a_peer(d))
        )

    def to_copy(j):
        return remote(
            tgt_out.at[j], tgt_in.at[me_b], to_send.at[0], to_recv.at[0], b_device(j)
        )

    each(1, n_a, lambda d: a_copy(d, me_a).start())
    each(0, top, lambda j: when(j < me_b, lambda: t_down(j).start()))

    def t_wait(j):
        t_copy(me_b, j, t_send.at[0, j]).wait_recv()

    def hand_up(j):
        when(j < me_b, lambda: t_wait(j))
        when((j <= me_b) & (me_b < top), lambda: t_up(j).start())

    each(0, top, hand_up)

    wait_all(a_slots, a_recv)
    for a in range(n_a):
        row_stack[a * rows : a * rows + split, :] = a_slots[a, :, 0:stack]
        row_stack[a * rows + split : (a + 1) * rows, :] = a_slots[
            a, 0 : rows - split, stack : 2 * stack
        ]
    col_stack[...] = row_stack[...].T

    def block(d):
        first = isinstance(d, int) and d == 0
        when(d > me_b, lambda: t_wait(d))
        points = t_slots[d]
        cols = points.shape[1]
        zero_low = jnp.zeros((head, cols), jnp.bfloat16)
        zero_high = jnp.zeros((k, cols), jnp.bfloat16)
        rhs = jnp.concatenate(
            [
                jnp.concatenate([points[0:head], zero_high], 0),
                jnp.concatenate([zero_low, points[head:]], 0),
            ],
            1,
        )
        both = jnp.dot(row_stack[...], rhs, preferred_element_type=jnp.float32)
        squared, plan = both[:, 0:cols], both[:, cols:]
        inv = lax.rsqrt(squared)
        terms = jnp.concatenate(
            [(plan * inv).astype(jnp.bfloat16), (squared * inv).astype(jnp.bfloat16)], 1
        )
        col = jnp.dot(col_stack[...], terms, preferred_element_type=jnp.float32)
        mass = col[f + 3 : f + 4, 0:cols]
        tgt_out[d, 0:f, :] = points[0:f].astype(jnp.float32) * mass + 0.5 * col[0:f, 0:cols]
        tgt_out[d, f:, :] = col[head:, cols:]
        when(d != me_b, lambda: to_copy(d).start())
        row = lax.dot_general(terms, rhs, NT, preferred_element_type=jnp.float32)
        if first:
            row_acc[...] = row
        else:
            row_acc[...] += row

    block(0)
    each(1, n_b, block)

    def pack(d):
        start = pl.multiple_of(a_peer(d) * rows, 8)
        src_out[d, :, 0:stack] = row_acc[pl.ds(start, half), :]
        src_out[d, :, stack : 2 * stack] = row_acc[pl.ds(start + half, half), :]
        so_copy(d, me_a).start()

    each(1, n_a, pack)
    mine = pl.multiple_of(me_a * rows, 8)
    src_out[0, :, 0:stack] = row_acc[pl.ds(mine, half), :]
    src_out[0, :, stack : 2 * stack] = row_acc[pl.ds(mine + half, half), :]

    wait_all(tgt_in, to_recv)
    total = fold(1, n_b, tgt_out[me_b], lambda d, sum_: sum_ + tgt_in[b_peer(d)])
    gy_ref[...] = total[0:f] * scale
    gr_ref[...] = total[f:] * inverse_g * scale

    wait_all(src_in, so_recv)
    total = fold(1, n_a, src_out[0], lambda d, sum_: sum_ + src_in[a_peer(d)])
    total = jnp.concatenate([total[:, 0:stack], total[:, stack : 2 * stack]], 0).T
    gx_ref[...] = (x * total[f : f + 1] - total[0:f]) * scale
    gq_ref[...] = total[head:] * scale

    wait_all(a_slots, a_send)
    each(0, top, lambda j: when(j < me_b, lambda: t_down(j).wait_send()))
    each(0, top, lambda j: when((j <= me_b) & (me_b < top), lambda: t_up(j).wait_send()))
    wait_all(src_out, so_send)
    wait_all(tgt_out, to_send)


def place(*refs):
    sources, places, sems = refs[0:4], refs[4:8], refs[8]
    copies = [
        pltpu.make_async_copy(src, dst, sems.at[i])
        for i, (src, dst) in enumerate(zip(sources, places))
    ]
    for copy in copies:
        copy.start()
    for copy in copies:
        copy.wait()


def local(src_feats, src_factor, tgt_feats, tgt_factor, rank_weight):
    n_src = lax.axis_size("src")
    n_tgt = lax.axis_size("tgt")
    low = 2 if n_tgt % 2 == 0 else 1
    n_a, n_b = n_src * low, n_tgt // low
    f, rows = src_feats.shape
    k = src_factor.shape[0]
    cols = tgt_feats.shape[1]
    stack = f + AUG + k
    split = (rows // 2 + 15) // 16 * 16
    f32, bf16 = jnp.float32, jnp.bfloat16
    scale = 1.0 / (cols * n_src * n_tgt)
    vmem = pl.BlockSpec(memory_space=pltpu.VMEM)
    hbm = pl.BlockSpec(memory_space=pltpu.HBM)
    dma = pltpu.SemaphoreType.DMA
    out_shape = (
        jax.ShapeDtypeStruct((f, rows), f32),
        jax.ShapeDtypeStruct((k, rows), f32),
        jax.ShapeDtypeStruct((f, cols), f32),
        jax.ShapeDtypeStruct((k, cols), f32),
    )
    results = pl.pallas_call(
        functools.partial(kernel, n_src, n_tgt, low, scale),
        out_shape=tuple(pltpu.VMEM(o.shape, o.dtype) for o in out_shape),
        in_specs=[hbm] * 5,
        out_specs=(vmem,) * 4,
        scratch_shapes=[
            pltpu.VMEM((f, rows), bf16),
            pltpu.VMEM((k, rows), bf16),
            pltpu.VMEM((f, cols), bf16),
            pltpu.VMEM((k, cols), bf16),
            pltpu.VMEM((1, k), f32),
            pltpu.VMEM((n_a, split, 2 * stack), bf16),
            pltpu.VMEM((n_b, stack, cols), bf16),
            pltpu.VMEM((n_a * rows, stack), bf16),
            pltpu.VMEM((stack, n_a * rows), bf16),
            pltpu.VMEM((n_a * rows, stack), f32),
            pltpu.VMEM((n_a, rows // 2, 2 * stack), f32),
            pltpu.VMEM((n_a, rows // 2, 2 * stack), f32),
            pltpu.VMEM((n_b, f + k, cols), f32),
            pltpu.VMEM((n_b, f + k, cols), f32),
            dma((5,)),
            dma((n_a,)),
            dma((n_a,)),
            dma((2, n_b)),
            dma((n_b,)),
            dma((n_a,)),
            dma((n_a,)),
            dma((n_b,)),
            dma((n_b,)),
        ],
        compiler_params=pltpu.CompilerParams(
            collective_id=0, has_side_effects=True, vmem_limit_bytes=63 * 1024 * 1024
        ),
    )(src_feats, src_factor, tgt_feats, tgt_factor, rank_weight.reshape(1, k))
    return pl.pallas_call(
        place,
        out_shape=out_shape,
        in_specs=[vmem] * 4,
        out_specs=(hbm,) * 4,
        scratch_shapes=[dma((4,))],
    )(*(pltpu.with_memory_space_constraint(r, pltpu.VMEM) for r in results))


def solution(mesh):
    src = P(None, ("src", "tgt"))
    tgt = P(None, ("tgt", "src"))
    return jax.shard_map(
        local,
        mesh=mesh,
        in_specs=(src, src, tgt, tgt, P()),
        out_specs=(src, src, tgt, tgt),
        check_vma=False,
    )
```

```python
import functools

import jax
import jax.numpy as jnp
from jax import lax
from jax.experimental import pallas as pl
from jax.experimental.pallas import tpu as pltpu
from jax.sharding import PartitionSpec as P

MESH = pl.DeviceIdType.MESH
NT = (((1,), (1,)), ((), ()))
AUG = 16


def each(low, high, body):
    if high - low <= 8:
        for i in range(low, high):
            body(i)
    else:
        lax.fori_loop(low, high, lambda i, c: (body(i), c)[1], 0)


def fold(low, high, start, body):
    if high - low <= 8:
        for i in range(low, high):
            start = body(i, start)
        return start
    return lax.fori_loop(low, high, body, start)


def split3(value):
    high = value.astype(jnp.bfloat16).astype(jnp.float32)
    rest = value - high
    mid = rest.astype(jnp.bfloat16).astype(jnp.float32)
    return high, mid, rest - mid


def aug_rows(feats, first, ones_at, extra):
    norm = jnp.sum(feats * feats, axis=0, keepdims=True) + extra
    high, mid, low = split3(norm)
    shape = (AUG, feats.shape[1])
    row = lax.broadcasted_iota(jnp.int32, shape, 0)
    out = jnp.where((row >= ones_at) & (row < ones_at + 3), 1.0, 0.0)
    for k, part in enumerate((high, mid, low)):
        out = jnp.where(row == first + k, jnp.broadcast_to(part, shape), out)
    return out


def kernel(
    n_src, n_tgt, low, scale,
    x_hbm, q_hbm, y_hbm, r_hbm, g_hbm,
    gx_ref, gq_ref, gy_ref, gr_ref,
    x_in, q_in, y_in, r_in, g_in,
    a_slots, t_slots, row_stack, col_stack, row_acc, last_terms,
    src_out, src_in, tgt_out, tgt_in,
    load_sem, a_send, a_recv, t_send, t_recv, so_send, so_recv, to_send, to_recv,
):
    f, rows = x_in.shape
    k = q_in.shape[0]
    head = f + AUG
    stack = head + k
    half = rows // 2
    split = a_slots.shape[1]
    n_a = n_src * low
    n_b = n_tgt // low
    me_s = lax.axis_index("src")
    me_t = lax.axis_index("tgt")
    me_b = me_t // low
    me_low = me_t % low
    me_a = me_s * low + me_low

    def a_peer(d):
        return lax.rem(me_a + d, n_a)

    def b_peer(d):
        if n_b & (n_b - 1) or n_b > 8:
            return lax.rem(me_b + d, n_b)
        peer, bit = me_b, 1
        while bit <= d:
            if d & bit:
                peer = peer + bit - 2 * bit * ((peer // bit) % 2)
            bit *= 2
        return peer

    def a_device(a):
        return {"src": a // low, "tgt": me_b * low + a % low}

    def b_device(b):
        return {"src": me_s, "tgt": b * low + me_low}

    loads = [
        pltpu.make_async_copy(src, dst, load_sem.at[i])
        for i, (src, dst) in enumerate(
            ((x_hbm, x_in), (q_hbm, q_in), (y_hbm, y_in), (r_hbm, r_in), (g_hbm, g_in))
        )
    ]
    for load in loads:
        load.start()

    barrier = pltpu.get_barrier_semaphore()

    def greet(device):
        pl.semaphore_signal(barrier, inc=1, device_id=device, device_id_type=MESH)

    each(1, n_a, lambda d: greet(a_device(a_peer(d))))
    each(1, n_b, lambda d: greet(b_device(b_peer(d))))

    for load in loads:
        load.wait()

    x = x_in[...].astype(jnp.float32)
    mine = jnp.concatenate([x * -2.0, aug_rows(x, 0, 3, 0.0), q_in[...].astype(jnp.float32)], 0)
    mine = mine.T.astype(jnp.bfloat16)
    a_slots[me_a, :, 0:stack] = mine[0:split]
    a_slots[me_a, 0 : rows - split, stack : 2 * stack] = mine[split:]
    inv_row = 1.0 / g_in[...]
    square = (k, k)
    diagonal = lax.broadcasted_iota(jnp.int32, square, 0) == lax.broadcasted_iota(
        jnp.int32, square, 1
    )
    inverse_g = jnp.sum(
        jnp.where(diagonal, jnp.broadcast_to(inv_row, square), 0.0), axis=1, keepdims=True
    )
    y = y_in[...]
    t_slots[me_b, 0:f, :] = y
    t_slots[me_b, f:head, :] = aug_rows(y.astype(jnp.float32), 3, 0, 1.0).astype(jnp.bfloat16)
    t_slots[me_b, head:, :] = (r_in[...].astype(jnp.float32) * inverse_g).astype(jnp.bfloat16)

    pl.semaphore_wait(barrier, n_a + n_b - 2)

    def remote(src, dst, send, recv, device):
        return pltpu.make_async_remote_copy(
            src_ref=src, dst_ref=dst, send_sem=send, recv_sem=recv,
            device_id=device, device_id_type=MESH,
        )

    def wait_all(slots, sem):
        ref = slots.at[pl.ds(0, slots.shape[0] - 1)]
        pltpu.make_async_copy(ref, ref, sem.at[0]).wait()

    def a_copy(d, slot):
        ref = a_slots.at[slot]
        return remote(ref, ref, a_send.at[0], a_recv.at[0], a_device(a_peer(d)))

    def t_copy(d, slot):
        ref = t_slots.at[slot]
        return remote(ref, ref, t_send.at[0], t_recv.at[slot], b_device(b_peer(d)))

    def so_copy(a):
        return remote(
            src_out.at[a], src_in.at[me_a], so_send.at[0], so_recv.at[0], a_device(a)
        )

    def to_copy(d, slot):
        return remote(
            tgt_out.at[d], tgt_in.at[slot], to_send.at[0], to_recv.at[0], b_device(b_peer(d))
        )

    each(1, n_a, lambda d: a_copy(d, me_a).start())
    each(1, n_b, lambda d: t_copy(d, me_b).start())

    wait_all(a_slots, a_recv)
    for a in range(n_a):
        row_stack[a * rows : a * rows + split, :] = a_slots[a, :, 0:stack]
        row_stack[a * rows + split : (a + 1) * rows, :] = a_slots[
            a, 0 : rows - split, stack : 2 * stack
        ]
    col_stack[...] = row_stack[...].T

    def right_side(peer):
        points = t_slots[peer]
        cols = points.shape[1]
        zero_low = jnp.zeros((head, cols), jnp.bfloat16)
        zero_high = jnp.zeros((k, cols), jnp.bfloat16)
        rhs = jnp.concatenate(
            [
                jnp.concatenate([points[0:head], zero_high], 0),
                jnp.concatenate([zero_low, points[head:]], 0),
            ],
            1,
        )
        return points, rhs

    def pair_terms(points, rhs):
        cols = rhs.shape[1] // 2
        both = jnp.dot(points, rhs, preferred_element_type=jnp.float32)
        squared, plan = both[:, 0:cols], both[:, cols:]
        inv = lax.rsqrt(squared)
        return jnp.concatenate(
            [(plan * inv).astype(jnp.bfloat16), (squared * inv).astype(jnp.bfloat16)], 1
        )

    def put_col(d, points, terms):
        cols = points.shape[1]
        col = jnp.dot(col_stack[...], terms, preferred_element_type=jnp.float32)
        mass = col[f + 3 : f + 4, 0:cols]
        tgt_out[d, 0:f, :] = points[0:f].astype(jnp.float32) * mass + 0.5 * col[0:f, 0:cols]
        tgt_out[d, f:, :] = col[head:, cols:]

    def block(d):
        first = isinstance(d, int) and d == 0
        peer = b_peer(d)
        if not first:
            t_copy(d, peer).wait_recv()
        points, rhs = right_side(peer)
        terms = pair_terms(row_stack[...], rhs)
        put_col(d, points, terms)
        if not first:
            to_copy(d, me_b).start()
        row = lax.dot_general(terms, rhs, NT, preferred_element_type=jnp.float32)
        if first:
            row_acc[...] = row
        else:
            row_acc[...] += row

    block(0)
    each(2, n_b, lambda d: block(n_b + 1 - d))

    t_copy(1, b_peer(1)).wait_recv()
    points, rhs = right_side(b_peer(1))
    group = 2 if n_a % 2 == 0 else 1
    mine = me_a // group

    def finish(c):
        base = lax.rem(mine + c, n_a // group) * group
        at = pl.ds(pl.multiple_of(base * rows, 16), group * rows)
        terms = pair_terms(row_stack[at, :], rhs)
        last_terms[at, :] = terms
        row = lax.dot_general(terms, rhs, NT, preferred_element_type=jnp.float32)
        row = row + row_acc[at, :]
        for i in range(group):
            a = base + i
            src_out[a, :, 0:stack] = row[i * rows : i * rows + half]
            src_out[a, :, stack : 2 * stack] = row[i * rows + half : (i + 1) * rows]

            @pl.when(a != me_a)
            def _():
                so_copy(a).start()

    each(1, n_a // group, finish)
    finish(0)
    put_col(1, points, last_terms[...])
    to_copy(1, me_b).start()

    wait_all(tgt_in, to_recv)
    total = fold(1, n_b, tgt_out[0], lambda d, sum_: sum_ + tgt_in[b_peer(d)])
    gy_ref[...] = total[0:f] * scale
    gr_ref[...] = total[f:] * inverse_g * scale

    wait_all(src_in, so_recv)
    total = fold(1, n_a, src_out[me_a], lambda d, sum_: sum_ + src_in[a_peer(d)])
    total = jnp.concatenate([total[:, 0:stack], total[:, stack : 2 * stack]], 0).T
    gx_ref[...] = (x * total[f : f + 1] - total[0:f]) * scale
    gq_ref[...] = total[head:] * scale

    wait_all(a_slots, a_send)
    wait_all(t_slots, t_send)
    wait_all(src_out, so_send)
    wait_all(tgt_out, to_send)


def place(*refs):
    sources, places, sems = refs[0:4], refs[4:8], refs[8]
    copies = [
        pltpu.make_async_copy(src, dst, sems.at[i])
        for i, (src, dst) in enumerate(zip(sources, places))
    ]
    for copy in copies:
        copy.start()
    for copy in copies:
        copy.wait()


def local(src_feats, src_factor, tgt_feats, tgt_factor, rank_weight):
    n_src = lax.axis_size("src")
    n_tgt = lax.axis_size("tgt")
    low = 2 if n_tgt % 2 == 0 else 1
    n_a, n_b = n_src * low, n_tgt // low
    f, rows = src_feats.shape
    k = src_factor.shape[0]
    cols = tgt_feats.shape[1]
    stack = f + AUG + k
    split = (rows // 2 + 15) // 16 * 16
    f32, bf16 = jnp.float32, jnp.bfloat16
    scale = 1.0 / (cols * n_src * n_tgt)
    vmem = pl.BlockSpec(memory_space=pltpu.VMEM)
    hbm = pl.BlockSpec(memory_space=pltpu.HBM)
    dma = pltpu.SemaphoreType.DMA
    out_shape = (
        jax.ShapeDtypeStruct((f, rows), f32),
        jax.ShapeDtypeStruct((k, rows), f32),
        jax.ShapeDtypeStruct((f, cols), f32),
        jax.ShapeDtypeStruct((k, cols), f32),
    )
    results = pl.pallas_call(
        functools.partial(kernel, n_src, n_tgt, low, scale),
        out_shape=tuple(pltpu.VMEM(o.shape, o.dtype) for o in out_shape),
        in_specs=[hbm] * 5,
        out_specs=(vmem,) * 4,
        scratch_shapes=[
            pltpu.VMEM((f, rows), bf16),
            pltpu.VMEM((k, rows), bf16),
            pltpu.VMEM((f, cols), bf16),
            pltpu.VMEM((k, cols), bf16),
            pltpu.VMEM((1, k), f32),
            pltpu.VMEM((n_a, split, 2 * stack), bf16),
            pltpu.VMEM((n_b, stack, cols), bf16),
            pltpu.VMEM((n_a * rows, stack), bf16),
            pltpu.VMEM((stack, n_a * rows), bf16),
            pltpu.VMEM((n_a * rows, stack), f32),
            pltpu.VMEM((n_a * rows, 2 * cols), bf16),
            pltpu.VMEM((n_a, rows // 2, 2 * stack), f32),
            pltpu.VMEM((n_a, rows // 2, 2 * stack), f32),
            pltpu.VMEM((n_b, f + k, cols), f32),
            pltpu.VMEM((n_b, f + k, cols), f32),
            dma((5,)),
            dma((n_a,)),
            dma((n_a,)),
            dma((n_b,)),
            dma((n_b,)),
            dma((n_a,)),
            dma((n_a,)),
            dma((n_b,)),
            dma((n_b,)),
        ],
        compiler_params=pltpu.CompilerParams(
            collective_id=0, has_side_effects=True, vmem_limit_bytes=63 * 1024 * 1024
        ),
    )(src_feats, src_factor, tgt_feats, tgt_factor, rank_weight.reshape(1, k))
    return pl.pallas_call(
        place,
        out_shape=out_shape,
        in_specs=[vmem] * 4,
        out_specs=(hbm,) * 4,
        scratch_shapes=[dma((4,))],
    )(*(pltpu.with_memory_space_constraint(r, pltpu.VMEM) for r in results))


def solution(mesh):
    src = P(None, ("src", "tgt"))
    tgt = P(None, ("tgt", "src"))
    return jax.shard_map(
        local,
        mesh=mesh,
        in_specs=(src, src, tgt, tgt, P()),
        out_specs=(src, src, tgt, tgt),
        check_vma=False,
    )
```

```python
import functools

import jax
import jax.numpy as jnp
from jax import lax
from jax.experimental import pallas as pl
from jax.experimental.pallas import tpu as pltpu
from jax.sharding import PartitionSpec as P

MESH = pl.DeviceIdType.MESH
NT = (((1,), (1,)), ((), ()))
AUG = 16


def each(low, high, body):
    lax.fori_loop(low, high, lambda i, c: (body(i), c)[1], 0)


def fold(low, high, start, body):
    return lax.fori_loop(low, high, body, start)


def split3(value):
    high = value.astype(jnp.bfloat16).astype(jnp.float32)
    rest = value - high
    mid = rest.astype(jnp.bfloat16).astype(jnp.float32)
    return high, mid, rest - mid


def aug_rows(feats, first, ones_at, extra):
    norm = jnp.sum(feats * feats, axis=0, keepdims=True) + extra
    high, mid, low = split3(norm)
    shape = (AUG, feats.shape[1])
    row = lax.broadcasted_iota(jnp.int32, shape, 0)
    out = jnp.where((row >= ones_at) & (row < ones_at + 3), 1.0, 0.0)
    for k, part in enumerate((high, mid, low)):
        out = jnp.where(row == first + k, jnp.broadcast_to(part, shape), out)
    return out


def kernel(
    n_src, n_tgt, low, scale,
    x_hbm, q_hbm, y_hbm, r_hbm, g_hbm,
    gx_ref, gq_ref, gy_ref, gr_ref,
    x_in, q_in, y_in, r_in, g_in,
    a_slots, t_slots, row_stack, col_stack, row_acc,
    src_out, src_in, tgt_out, tgt_in,
    load_sem, a_send, a_recv, t_send, t_recv, so_send, so_recv, to_send, to_recv,
):
    f, rows = x_in.shape
    k = q_in.shape[0]
    head = f + AUG
    stack = head + k
    half = rows // 2
    split = a_slots.shape[1]
    n_a = n_src * low
    n_b = n_tgt // low
    me_s = lax.axis_index("src")
    me_t = lax.axis_index("tgt")
    me_b = me_t // low
    me_low = me_t % low
    me_a = me_s * low + me_low

    def a_peer(d):
        return lax.rem(me_a + d, n_a)

    def b_peer(d):
        if n_b & (n_b - 1):
            return lax.rem(me_b + d, n_b)
        peer, bit = 0, 1
        while bit < n_b:
            peer = peer + bit * ((me_b // bit + d // bit) % 2)
            bit *= 2
        return peer

    def a_device(a):
        return {"src": a // low, "tgt": me_b * low + a % low}

    def b_device(b):
        return {"src": me_s, "tgt": b * low + me_low}

    loads = [
        pltpu.make_async_copy(src, dst, load_sem.at[i])
        for i, (src, dst) in enumerate(
            ((x_hbm, x_in), (q_hbm, q_in), (y_hbm, y_in), (r_hbm, r_in), (g_hbm, g_in))
        )
    ]
    for load in loads:
        load.start()

    barrier = pltpu.get_barrier_semaphore()

    def greet(device):
        pl.semaphore_signal(barrier, inc=1, device_id=device, device_id_type=MESH)

    each(1, n_a, lambda d: greet(a_device(a_peer(d))))
    each(1, n_b, lambda d: greet(b_device(b_peer(d))))

    for load in loads:
        load.wait()

    x = x_in[...].astype(jnp.float32)
    mine = jnp.concatenate([x * -2.0, aug_rows(x, 0, 3, 0.0), q_in[...].astype(jnp.float32)], 0)
    mine = mine.T.astype(jnp.bfloat16)
    a_slots[me_a, :, 0:stack] = mine[0:split]
    a_slots[me_a, 0 : rows - split, stack : 2 * stack] = mine[split:]
    inv_row = 1.0 / g_in[...]
    square = (k, k)
    diagonal = lax.broadcasted_iota(jnp.int32, square, 0) == lax.broadcasted_iota(
        jnp.int32, square, 1
    )
    inverse_g = jnp.sum(
        jnp.where(diagonal, jnp.broadcast_to(inv_row, square), 0.0), axis=1, keepdims=True
    )
    y = y_in[...]
    t_slots[me_b, 0:f, :] = y
    t_slots[me_b, f:head, :] = aug_rows(y.astype(jnp.float32), 3, 0, 1.0).astype(jnp.bfloat16)
    t_slots[me_b, head:, :] = (r_in[...].astype(jnp.float32) * inverse_g).astype(jnp.bfloat16)

    pl.semaphore_wait(barrier, n_a + n_b - 2)

    def remote(src, dst, send, recv, device):
        return pltpu.make_async_remote_copy(
            src_ref=src, dst_ref=dst, send_sem=send, recv_sem=recv,
            device_id=device, device_id_type=MESH,
        )

    def wait_all(slots, sem):
        ref = slots.at[pl.ds(0, slots.shape[0] - 1)]
        pltpu.make_async_copy(ref, ref, sem.at[0]).wait()

    def a_copy(d, slot):
        ref = a_slots.at[slot]
        return remote(ref, ref, a_send.at[0], a_recv.at[0], a_device(a_peer(d)))

    def t_copy(d, slot):
        ref = t_slots.at[slot]
        return remote(ref, ref, t_send.at[0], t_recv.at[slot], b_device(b_peer(d)))

    def so_copy(d, slot):
        return remote(
            src_out.at[d], src_in.at[slot], so_send.at[0], so_recv.at[0], a_device(a_peer(d))
        )

    def to_copy(d, slot):
        return remote(
            tgt_out.at[d], tgt_in.at[slot], to_send.at[0], to_recv.at[0], b_device(b_peer(d))
        )

    each(1, n_a, lambda d: a_copy(d, me_a).start())
    each(1, n_b, lambda d: t_copy(d, me_b).start())

    wait_all(a_slots, a_recv)
    row_acc[...] = jnp.zeros_like(row_acc)

    def unpack(a):
        start = pl.multiple_of(a * rows, 16)
        row_stack[pl.ds(start, split), :] = a_slots[a, :, 0:stack]
        row_stack[pl.ds(start + split, rows - split), :] = a_slots[
            a, 0 : rows - split, stack : 2 * stack
        ]

    each(0, n_a, unpack)
    col_stack[...] = row_stack[...].T

    def block(d):
        peer = b_peer(d)

        @pl.when(d > 0)
        def _():
            t_copy(d, peer).wait_recv()

        points = t_slots[peer]
        cols = points.shape[1]
        zero_low = jnp.zeros((head, cols), jnp.bfloat16)
        zero_high = jnp.zeros((k, cols), jnp.bfloat16)
        rhs = jnp.concatenate(
            [
                jnp.concatenate([points[0:head], zero_high], 0),
                jnp.concatenate([zero_low, points[head:]], 0),
            ],
            1,
        )
        both = jnp.dot(row_stack[...], rhs, preferred_element_type=jnp.float32)
        squared, plan = both[:, 0:cols], both[:, cols:]
        inv = lax.rsqrt(squared)
        terms = jnp.concatenate(
            [(plan * inv).astype(jnp.bfloat16), (squared * inv).astype(jnp.bfloat16)], 1
        )
        col = jnp.dot(col_stack[...], terms, preferred_element_type=jnp.float32)
        mass = col[f + 3 : f + 4, 0:cols]
        tgt_out[d, 0:f, :] = points[0:f].astype(jnp.float32) * mass + 0.5 * col[0:f, 0:cols]
        tgt_out[d, f:, :] = col[head:, cols:]

        @pl.when(d > 0)
        def _():
            to_copy(d, me_b).start()

        row = lax.dot_general(terms, rhs, NT, preferred_element_type=jnp.float32)
        row_acc[...] += row

    each(0, n_b, block)

    def pack(d):
        start = pl.multiple_of(a_peer(d) * rows, 8)
        src_out[d, :, 0:stack] = row_acc[pl.ds(start, half), :]
        src_out[d, :, stack : 2 * stack] = row_acc[pl.ds(start + half, half), :]
        so_copy(d, me_a).start()

    each(1, n_a, pack)
    mine = pl.multiple_of(me_a * rows, 8)
    src_out[0, :, 0:stack] = row_acc[pl.ds(mine, half), :]
    src_out[0, :, stack : 2 * stack] = row_acc[pl.ds(mine + half, half), :]

    wait_all(tgt_in, to_recv)
    total = fold(1, n_b, tgt_out[0], lambda d, sum_: sum_ + tgt_in[b_peer(d)])
    gy_ref[...] = total[0:f] * scale
    gr_ref[...] = total[f:] * inverse_g * scale

    wait_all(src_in, so_recv)
    total = fold(1, n_a, src_out[0], lambda d, sum_: sum_ + src_in[a_peer(d)])
    total = jnp.concatenate([total[:, 0:stack], total[:, stack : 2 * stack]], 0).T
    gx_ref[...] = (x * total[f : f + 1] - total[0:f]) * scale
    gq_ref[...] = total[head:] * scale

    wait_all(a_slots, a_send)
    wait_all(t_slots, t_send)
    wait_all(src_out, so_send)
    wait_all(tgt_out, to_send)


def place(*refs):
    sources, places, sems = refs[0:4], refs[4:8], refs[8]
    copies = [
        pltpu.make_async_copy(src, dst, sems.at[i])
        for i, (src, dst) in enumerate(zip(sources, places))
    ]
    for copy in copies:
        copy.start()
    for copy in copies:
        copy.wait()


def local(src_feats, src_factor, tgt_feats, tgt_factor, rank_weight):
    n_src = lax.axis_size("src")
    n_tgt = lax.axis_size("tgt")
    low = 2 if n_tgt % 2 == 0 else 1
    n_a, n_b = n_src * low, n_tgt // low
    f, rows = src_feats.shape
    k = src_factor.shape[0]
    cols = tgt_feats.shape[1]
    stack = f + AUG + k
    split = (rows // 2 + 15) // 16 * 16
    f32, bf16 = jnp.float32, jnp.bfloat16
    scale = 1.0 / (cols * n_src * n_tgt)
    vmem = pl.BlockSpec(memory_space=pltpu.VMEM)
    hbm = pl.BlockSpec(memory_space=pltpu.HBM)
    dma = pltpu.SemaphoreType.DMA
    out_shape = (
        jax.ShapeDtypeStruct((f, rows), f32),
        jax.ShapeDtypeStruct((k, rows), f32),
        jax.ShapeDtypeStruct((f, cols), f32),
        jax.ShapeDtypeStruct((k, cols), f32),
    )
    results = pl.pallas_call(
        functools.partial(kernel, n_src, n_tgt, low, scale),
        out_shape=tuple(pltpu.VMEM(o.shape, o.dtype) for o in out_shape),
        in_specs=[hbm] * 5,
        out_specs=(vmem,) * 4,
        scratch_shapes=[
            pltpu.VMEM((f, rows), bf16),
            pltpu.VMEM((k, rows), bf16),
            pltpu.VMEM((f, cols), bf16),
            pltpu.VMEM((k, cols), bf16),
            pltpu.VMEM((1, k), f32),
            pltpu.VMEM((n_a, split, 2 * stack), bf16),
            pltpu.VMEM((n_b, stack, cols), bf16),
            pltpu.VMEM((n_a * rows, stack), bf16),
            pltpu.VMEM((stack, n_a * rows), bf16),
            pltpu.VMEM((n_a * rows, stack), f32),
            pltpu.VMEM((n_a, rows // 2, 2 * stack), f32),
            pltpu.VMEM((n_a, rows // 2, 2 * stack), f32),
            pltpu.VMEM((n_b, f + k, cols), f32),
            pltpu.VMEM((n_b, f + k, cols), f32),
            dma((5,)),
            dma((n_a,)),
            dma((n_a,)),
            dma((n_b,)),
            dma((n_b,)),
            dma((n_a,)),
            dma((n_a,)),
            dma((n_b,)),
            dma((n_b,)),
        ],
        compiler_params=pltpu.CompilerParams(
            collective_id=0, has_side_effects=True, vmem_limit_bytes=63 * 1024 * 1024
        ),
    )(src_feats, src_factor, tgt_feats, tgt_factor, rank_weight.reshape(1, k))
    return pl.pallas_call(
        place,
        out_shape=out_shape,
        in_specs=[vmem] * 4,
        out_specs=(hbm,) * 4,
        scratch_shapes=[dma((4,))],
    )(*(pltpu.with_memory_space_constraint(r, pltpu.VMEM) for r in results))


def solution(mesh):
    src = P(None, ("src", "tgt"))
    tgt = P(None, ("tgt", "src"))
    return jax.shard_map(
        local,
        mesh=mesh,
        in_specs=(src, src, tgt, tgt, P()),
        out_specs=(src, src, tgt, tgt),
        check_vma=False,
    )
```

```python
import functools

import jax
import jax.numpy as jnp
from jax import lax
from jax.experimental import pallas as pl
from jax.experimental.pallas import tpu as pltpu
from jax.sharding import PartitionSpec as P

MESH = pl.DeviceIdType.MESH
NT = (((1,), (1,)), ((), ()))
AUG = 16


def each(low, high, body):
    if high - low <= 8:
        for i in range(low, high):
            body(i)
    else:
        lax.fori_loop(low, high, lambda i, c: (body(i), c)[1], 0)


def fold(low, high, start, body):
    if high - low <= 8:
        for i in range(low, high):
            start = body(i, start)
        return start
    return lax.fori_loop(low, high, body, start)


def add(total, part):
    return part if total is None else total + part


def split3(value):
    high = value.astype(jnp.bfloat16).astype(jnp.float32)
    rest = value - high
    mid = rest.astype(jnp.bfloat16).astype(jnp.float32)
    return high, mid, rest - mid


def aug_rows(feats, first, ones_at, extra):
    norm = jnp.sum(feats * feats, axis=0, keepdims=True) + extra
    high, mid, low = split3(norm)
    shape = (AUG, feats.shape[1])
    row = lax.broadcasted_iota(jnp.int32, shape, 0)
    out = jnp.where((row >= ones_at) & (row < ones_at + 3), 1.0, 0.0)
    for k, part in enumerate((high, mid, low)):
        out = jnp.where(row == first + k, jnp.broadcast_to(part, shape), out)
    return out


def kernel(
    n_src, n_tgt, low, scale,
    x_hbm, q_hbm, y_hbm, r_hbm, g_hbm,
    gx_ref, gq_ref, gy_ref, gr_ref,
    x_in, q_in, y_in, r_in, g_in,
    a_slots, t_slots, row_stack, col_stack, row_acc,
    src_out, src_in, tgt_out, tgt_in,
    load_sem, a_send, a_recv, t_send, t_recv, so_send, so_recv, to_send, to_recv,
):
    f, rows = x_in.shape
    k = q_in.shape[0]
    head = f + AUG
    stack = head + k
    half = rows // 2
    split = a_slots.shape[1]
    n_a = n_src * low
    n_b = n_tgt // low
    me_s = lax.axis_index("src")
    me_t = lax.axis_index("tgt")
    me_b = me_t // low
    me_low = me_t % low
    me_a = me_s * low + me_low

    def a_peer(d):
        return lax.rem(me_a + d, n_a)

    def b_peer(d):
        if n_b & (n_b - 1) or n_b > 8:
            return lax.rem(me_b + d, n_b)
        peer, bit = me_b, 1
        while bit <= d:
            if d & bit:
                peer = peer + bit - 2 * bit * ((peer // bit) % 2)
            bit *= 2
        return peer

    def a_device(a):
        return {"src": a // low, "tgt": me_b * low + a % low}

    def b_device(b):
        return {"src": me_s, "tgt": b * low + me_low}

    loads = [
        pltpu.make_async_copy(src, dst, load_sem.at[i])
        for i, (src, dst) in enumerate(
            ((x_hbm, x_in), (q_hbm, q_in), (y_hbm, y_in), (r_hbm, r_in), (g_hbm, g_in))
        )
    ]
    for load in loads:
        load.start()

    barrier = pltpu.get_barrier_semaphore()

    def greet(device):
        pl.semaphore_signal(barrier, inc=1, device_id=device, device_id_type=MESH)

    each(1, n_a, lambda d: greet(a_device(a_peer(d))))
    each(1, n_b, lambda d: greet(b_device(b_peer(d))))

    for load in loads:
        load.wait()

    x = x_in[...].astype(jnp.float32)
    mine = jnp.concatenate([x * -2.0, aug_rows(x, 0, 3, 0.0), q_in[...].astype(jnp.float32)], 0)
    mine = mine.T.astype(jnp.bfloat16)
    a_slots[me_a, :, 0:stack] = mine[0:split]
    a_slots[me_a, 0 : rows - split, stack : 2 * stack] = mine[split:]
    inv_row = 1.0 / g_in[...]
    square = (k, k)
    diagonal = lax.broadcasted_iota(jnp.int32, square, 0) == lax.broadcasted_iota(
        jnp.int32, square, 1
    )
    inverse_g = jnp.sum(
        jnp.where(diagonal, jnp.broadcast_to(inv_row, square), 0.0), axis=1, keepdims=True
    )
    y = y_in[...]
    t_slots[me_b, 0:f, :] = y
    t_slots[me_b, f:head, :] = aug_rows(y.astype(jnp.float32), 3, 0, 1.0).astype(jnp.bfloat16)
    t_slots[me_b, head:, :] = (r_in[...].astype(jnp.float32) * inverse_g).astype(jnp.bfloat16)

    pl.semaphore_wait(barrier, n_a + n_b - 2)

    def remote(src, dst, send, recv, device):
        return pltpu.make_async_remote_copy(
            src_ref=src, dst_ref=dst, send_sem=send, recv_sem=recv,
            device_id=device, device_id_type=MESH,
        )

    def wait_all(slots, sem):
        ref = slots.at[pl.ds(0, slots.shape[0] - 1)]
        pltpu.make_async_copy(ref, ref, sem.at[0]).wait()

    def a_copy(d, slot):
        ref = a_slots.at[slot]
        return remote(ref, ref, a_send.at[0], a_recv.at[0], a_device(a_peer(d)))

    def t_copy(d, slot):
        ref = t_slots.at[slot]
        return remote(ref, ref, t_send.at[0], t_recv.at[slot], b_device(b_peer(d)))

    def so_copy(d, slot):
        return remote(
            src_out.at[d], src_in.at[slot], so_send.at[0], so_recv.at[0], a_device(a_peer(d))
        )

    def to_copy(d, slot):
        return remote(
            tgt_out.at[d], tgt_in.at[slot], to_send.at[0], to_recv.at[0], b_device(b_peer(d))
        )

    each(1, n_a, lambda d: a_copy(d, me_a).start())
    each(1, n_b, lambda d: t_copy(d, me_b).start())

    wait_all(a_slots, a_recv)
    for a in range(n_a):
        row_stack[a * rows : a * rows + split, :] = a_slots[a, :, 0:stack]
        row_stack[a * rows + split : (a + 1) * rows, :] = a_slots[
            a, 0 : rows - split, stack : 2 * stack
        ]
    col_stack[...] = row_stack[...].T

    def blocks(several):
        parts = []
        for d in several:
            peer = b_peer(d)
            if not (isinstance(d, int) and d == 0):
                t_copy(d, peer).wait_recv()
            parts.append(t_slots[peer])
        cols = parts[0].shape[1]
        wide = cols * len(parts)
        zero_low = jnp.zeros((head, cols), jnp.bfloat16)
        zero_high = jnp.zeros((k, cols), jnp.bfloat16)
        rhs = jnp.concatenate(
            [jnp.concatenate([p[0:head], zero_high], 0) for p in parts]
            + [jnp.concatenate([zero_low, p[head:]], 0) for p in parts],
            1,
        )
        both = jnp.dot(row_stack[...], rhs, preferred_element_type=jnp.float32)
        squared, plan = both[:, 0:wide], both[:, wide:]
        inv = lax.rsqrt(squared)
        terms = jnp.concatenate(
            [(plan * inv).astype(jnp.bfloat16), (squared * inv).astype(jnp.bfloat16)], 1
        )
        col = jnp.dot(col_stack[...], terms, preferred_element_type=jnp.float32)
        for i, d in enumerate(several):
            at = slice(i * cols, (i + 1) * cols)
            mass = col[f + 3 : f + 4, at]
            tgt_out[d, 0:f, :] = parts[i][0:f].astype(jnp.float32) * mass + 0.5 * col[0:f, at]
            tgt_out[d, f:, :] = col[head:, wide + i * cols : wide + (i + 1) * cols]
            if not (isinstance(d, int) and d == 0):
                to_copy(d, me_b).start()
        return lax.dot_general(terms, rhs, NT, preferred_element_type=jnp.float32)

    size = 2 if n_b % 2 == 0 else 1
    row = fold(
        1, n_b // size, None,
        lambda g, sum_: add(sum_, blocks([g * size + i for i in range(size)])),
    ) if n_b // size <= 8 else None
    if row is None:
        row = lax.fori_loop(
            1, n_b // size,
            lambda g, sum_: sum_ + blocks([g * size + i for i in range(size)]),
            jnp.zeros_like(row_acc),
        )
    row_acc[...] = row + blocks(list(range(size)))

    def pack(d):
        start = pl.multiple_of(a_peer(d) * rows, 8)
        src_out[d, :, 0:stack] = row_acc[pl.ds(start, half), :]
        src_out[d, :, stack : 2 * stack] = row_acc[pl.ds(start + half, half), :]
        so_copy(d, me_a).start()

    each(1, n_a, pack)
    mine = pl.multiple_of(me_a * rows, 8)
    src_out[0, :, 0:stack] = row_acc[pl.ds(mine, half), :]
    src_out[0, :, stack : 2 * stack] = row_acc[pl.ds(mine + half, half), :]

    wait_all(tgt_in, to_recv)
    total = fold(1, n_b, tgt_out[0], lambda d, sum_: sum_ + tgt_in[b_peer(d)])
    gy_ref[...] = total[0:f] * scale
    gr_ref[...] = total[f:] * inverse_g * scale

    wait_all(src_in, so_recv)
    total = fold(1, n_a, src_out[0], lambda d, sum_: sum_ + src_in[a_peer(d)])
    total = jnp.concatenate([total[:, 0:stack], total[:, stack : 2 * stack]], 0).T
    gx_ref[...] = (x * total[f : f + 1] - total[0:f]) * scale
    gq_ref[...] = total[head:] * scale

    wait_all(a_slots, a_send)
    wait_all(t_slots, t_send)
    wait_all(src_out, so_send)
    wait_all(tgt_out, to_send)


def place(*refs):
    sources, places, sems = refs[0:4], refs[4:8], refs[8]
    copies = [
        pltpu.make_async_copy(src, dst, sems.at[i])
        for i, (src, dst) in enumerate(zip(sources, places))
    ]
    for copy in copies:
        copy.start()
    for copy in copies:
        copy.wait()


def local(src_feats, src_factor, tgt_feats, tgt_factor, rank_weight):
    n_src = lax.axis_size("src")
    n_tgt = lax.axis_size("tgt")
    low = 2 if n_tgt % 2 == 0 else 1
    n_a, n_b = n_src * low, n_tgt // low
    f, rows = src_feats.shape
    k = src_factor.shape[0]
    cols = tgt_feats.shape[1]
    stack = f + AUG + k
    split = (rows // 2 + 15) // 16 * 16
    f32, bf16 = jnp.float32, jnp.bfloat16
    scale = 1.0 / (cols * n_src * n_tgt)
    vmem = pl.BlockSpec(memory_space=pltpu.VMEM)
    hbm = pl.BlockSpec(memory_space=pltpu.HBM)
    dma = pltpu.SemaphoreType.DMA
    out_shape = (
        jax.ShapeDtypeStruct((f, rows), f32),
        jax.ShapeDtypeStruct((k, rows), f32),
        jax.ShapeDtypeStruct((f, cols), f32),
        jax.ShapeDtypeStruct((k, cols), f32),
    )
    results = pl.pallas_call(
        functools.partial(kernel, n_src, n_tgt, low, scale),
        out_shape=tuple(pltpu.VMEM(o.shape, o.dtype) for o in out_shape),
        in_specs=[hbm] * 5,
        out_specs=(vmem,) * 4,
        scratch_shapes=[
            pltpu.VMEM((f, rows), bf16),
            pltpu.VMEM((k, rows), bf16),
            pltpu.VMEM((f, cols), bf16),
            pltpu.VMEM((k, cols), bf16),
            pltpu.VMEM((1, k), f32),
            pltpu.VMEM((n_a, split, 2 * stack), bf16),
            pltpu.VMEM((n_b, stack, cols), bf16),
            pltpu.VMEM((n_a * rows, stack), bf16),
            pltpu.VMEM((stack, n_a * rows), bf16),
            pltpu.VMEM((n_a * rows, stack), f32),
            pltpu.VMEM((n_a, rows // 2, 2 * stack), f32),
            pltpu.VMEM((n_a, rows // 2, 2 * stack), f32),
            pltpu.VMEM((n_b, f + k, cols), f32),
            pltpu.VMEM((n_b, f + k, cols), f32),
            dma((5,)),
            dma((n_a,)),
            dma((n_a,)),
            dma((n_b,)),
            dma((n_b,)),
            dma((n_a,)),
            dma((n_a,)),
            dma((n_b,)),
            dma((n_b,)),
        ],
        compiler_params=pltpu.CompilerParams(
            collective_id=0, has_side_effects=True, vmem_limit_bytes=63 * 1024 * 1024
        ),
    )(src_feats, src_factor, tgt_feats, tgt_factor, rank_weight.reshape(1, k))
    return pl.pallas_call(
        place,
        out_shape=out_shape,
        in_specs=[vmem] * 4,
        out_specs=(hbm,) * 4,
        scratch_shapes=[dma((4,))],
    )(*(pltpu.with_memory_space_constraint(r, pltpu.VMEM) for r in results))


def solution(mesh):
    src = P(None, ("src", "tgt"))
    tgt = P(None, ("tgt", "src"))
    return jax.shard_map(
        local,
        mesh=mesh,
        in_specs=(src, src, tgt, tgt, P()),
        out_specs=(src, src, tgt, tgt),
        check_vma=False,
    )
```

```python
import functools

import jax
import jax.numpy as jnp
from jax import lax
from jax.experimental import pallas as pl
from jax.experimental.pallas import tpu as pltpu
from jax.sharding import PartitionSpec as P

MESH = pl.DeviceIdType.MESH
NT = (((1,), (1,)), ((), ()))
AUG = 16


def each(low, high, body):
    if high - low <= 8:
        for i in range(low, high):
            body(i)
    else:
        lax.fori_loop(low, high, lambda i, c: (body(i), c)[1], 0)


def fold(low, high, start, body):
    if high - low <= 8:
        for i in range(low, high):
            start = body(i, start)
        return start
    return lax.fori_loop(low, high, body, start)


def split3(value):
    high = value.astype(jnp.bfloat16).astype(jnp.float32)
    rest = value - high
    mid = rest.astype(jnp.bfloat16).astype(jnp.float32)
    return high, mid, rest - mid


def aug_rows(feats, first, ones_at, extra):
    norm = jnp.sum(feats * feats, axis=0, keepdims=True) + extra
    high, mid, low = split3(norm)
    shape = (AUG, feats.shape[1])
    row = lax.broadcasted_iota(jnp.int32, shape, 0)
    out = jnp.where((row >= ones_at) & (row < ones_at + 3), 1.0, 0.0)
    for k, part in enumerate((high, mid, low)):
        out = jnp.where(row == first + k, jnp.broadcast_to(part, shape), out)
    return out


def kernel(
    n_src, n_tgt, low, scale,
    x_hbm, q_hbm, y_hbm, r_hbm, g_hbm,
    gx_ref, gq_ref, gy_ref, gr_ref,
    x_in, q_in, y_in, r_in, g_in,
    a_slots, t_slots, row_stack, col_stack, row_acc,
    src_out, src_in, tgt_out, tgt_in,
    load_sem, a_send, a_recv, t_send, t_recv, so_send, so_recv, to_send, to_recv,
):
    f, rows = x_in.shape
    k = q_in.shape[0]
    head = f + AUG
    stack = head + k
    half = rows // 2
    split = a_slots.shape[1]
    n_a = n_src * low
    n_b = n_tgt // low
    me_s = lax.axis_index("src")
    me_t = lax.axis_index("tgt")
    me_b = me_t // low
    me_low = me_t % low
    me_a = me_s * low + me_low

    def a_peer(d):
        return lax.rem(me_a + d, n_a)

    def b_peer(d):
        if n_b & (n_b - 1) or n_b > 8:
            return lax.rem(me_b + d, n_b)
        peer, bit = me_b, 1
        while bit <= d:
            if d & bit:
                peer = peer + bit - 2 * bit * ((peer // bit) % 2)
            bit *= 2
        return peer

    def a_device(a):
        return {"src": a // low, "tgt": me_b * low + a % low}

    def b_device(b):
        return {"src": me_s, "tgt": b * low + me_low}

    loads = [
        pltpu.make_async_copy(src, dst, load_sem.at[i])
        for i, (src, dst) in enumerate(
            ((x_hbm, x_in), (q_hbm, q_in), (y_hbm, y_in), (r_hbm, r_in), (g_hbm, g_in))
        )
    ]
    for load in loads:
        load.start()

    barrier = pltpu.get_barrier_semaphore()

    def greet(device):
        pl.semaphore_signal(barrier, inc=1, device_id=device, device_id_type=MESH)

    each(1, n_a, lambda d: greet(a_device(a_peer(d))))
    each(1, n_b, lambda d: greet(b_device(b_peer(d))))

    for load in loads:
        load.wait()

    x = x_in[...].astype(jnp.float32)
    mine = jnp.concatenate([x * -2.0, aug_rows(x, 0, 3, 0.0), q_in[...].astype(jnp.float32)], 0)
    mine = mine.T.astype(jnp.bfloat16)
    a_slots[me_a, :, 0:stack] = mine[0:split]
    a_slots[me_a, 0 : rows - split, stack : 2 * stack] = mine[split:]
    inv_row = 1.0 / g_in[...]
    square = (k, k)
    diagonal = lax.broadcasted_iota(jnp.int32, square, 0) == lax.broadcasted_iota(
        jnp.int32, square, 1
    )
    inverse_g = jnp.sum(
        jnp.where(diagonal, jnp.broadcast_to(inv_row, square), 0.0), axis=1, keepdims=True
    )
    y = y_in[...]
    t_slots[me_b, 0:f, :] = y
    t_slots[me_b, f:head, :] = aug_rows(y.astype(jnp.float32), 3, 0, 1.0).astype(jnp.bfloat16)
    t_slots[me_b, head:, :] = (r_in[...].astype(jnp.float32) * inverse_g).astype(jnp.bfloat16)

    pl.semaphore_wait(barrier, n_a + n_b - 2)

    def remote(src, dst, send, recv, device):
        return pltpu.make_async_remote_copy(
            src_ref=src, dst_ref=dst, send_sem=send, recv_sem=recv,
            device_id=device, device_id_type=MESH,
        )

    def wait_all(slots, sem):
        ref = slots.at[pl.ds(0, slots.shape[0] - 1)]
        pltpu.make_async_copy(ref, ref, sem.at[0]).wait()

    def a_copy(d, slot):
        ref = a_slots.at[slot]
        return remote(ref, ref, a_send.at[0], a_recv.at[0], a_device(a_peer(d)))

    def t_copy(d, slot):
        ref = t_slots.at[slot]
        return remote(ref, ref, t_send.at[0], t_recv.at[slot], b_device(b_peer(d)))

    def so_copy(d, slot):
        return remote(
            src_out.at[d], src_in.at[slot], so_send.at[0], so_recv.at[0], a_device(a_peer(d))
        )

    def to_copy(d, slot):
        return remote(
            tgt_out.at[d], tgt_in.at[slot], to_send.at[0], to_recv.at[0], b_device(b_peer(d))
        )

    each(1, n_a, lambda d: a_copy(d, me_a).start())
    each(1, n_b, lambda d: t_copy(d, me_b).start())

    wait_all(a_slots, a_recv)
    for a in range(n_a):
        row_stack[a * rows : a * rows + split, :] = a_slots[a, :, 0:stack]
        row_stack[a * rows + split : (a + 1) * rows, :] = a_slots[
            a, 0 : rows - split, stack : 2 * stack
        ]
    col_stack[...] = row_stack[...].T

    def blocks(several):
        parts = []
        for d in several:
            peer = b_peer(d)
            if not (isinstance(d, int) and d == 0):
                t_copy(d, peer).wait_recv()
            parts.append(t_slots[peer])
        cols = parts[0].shape[1]
        wide = cols * len(parts)
        zero_low = jnp.zeros((head, cols), jnp.bfloat16)
        zero_high = jnp.zeros((k, cols), jnp.bfloat16)
        rhs = jnp.concatenate(
            [jnp.concatenate([p[0:head], zero_high], 0) for p in parts]
            + [jnp.concatenate([zero_low, p[head:]], 0) for p in parts],
            1,
        )
        both = jnp.dot(row_stack[...], rhs, preferred_element_type=jnp.float32)
        squared, plan = both[:, 0:wide], both[:, wide:]
        inv = lax.rsqrt(squared)
        terms = jnp.concatenate(
            [(plan * inv).astype(jnp.bfloat16), (squared * inv).astype(jnp.bfloat16)], 1
        )
        col = jnp.dot(col_stack[...], terms, preferred_element_type=jnp.float32)
        for i, d in enumerate(several):
            at = slice(i * cols, (i + 1) * cols)
            mass = col[f + 3 : f + 4, at]
            tgt_out[d, 0:f, :] = parts[i][0:f].astype(jnp.float32) * mass + 0.5 * col[0:f, at]
            tgt_out[d, f:, :] = col[head:, wide + i * cols : wide + (i + 1) * cols]
            if not (isinstance(d, int) and d == 0):
                to_copy(d, me_b).start()
        return lax.dot_general(terms, rhs, NT, preferred_element_type=jnp.float32)

    size = next(n for n in (4, 2, 1) if n_b % n == 0)
    if n_b // size <= 8:
        row = blocks(list(range(size)))
        for g in range(1, n_b // size):
            row = row + blocks([g * size + i for i in range(size)])
    else:
        row = lax.fori_loop(
            1, n_b // size,
            lambda g, sum_: sum_ + blocks([g * size + i for i in range(size)]),
            blocks(list(range(size))),
        )
    row_acc[...] = row

    def pack(d):
        start = pl.multiple_of(a_peer(d) * rows, 8)
        src_out[d, :, 0:stack] = row_acc[pl.ds(start, half), :]
        src_out[d, :, stack : 2 * stack] = row_acc[pl.ds(start + half, half), :]
        so_copy(d, me_a).start()

    each(1, n_a, pack)
    mine = pl.multiple_of(me_a * rows, 8)
    src_out[0, :, 0:stack] = row_acc[pl.ds(mine, half), :]
    src_out[0, :, stack : 2 * stack] = row_acc[pl.ds(mine + half, half), :]

    wait_all(tgt_in, to_recv)
    total = fold(1, n_b, tgt_out[0], lambda d, sum_: sum_ + tgt_in[b_peer(d)])
    gy_ref[...] = total[0:f] * scale
    gr_ref[...] = total[f:] * inverse_g * scale

    wait_all(src_in, so_recv)
    total = fold(1, n_a, src_out[0], lambda d, sum_: sum_ + src_in[a_peer(d)])
    total = jnp.concatenate([total[:, 0:stack], total[:, stack : 2 * stack]], 0).T
    gx_ref[...] = (x * total[f : f + 1] - total[0:f]) * scale
    gq_ref[...] = total[head:] * scale

    wait_all(a_slots, a_send)
    wait_all(t_slots, t_send)
    wait_all(src_out, so_send)
    wait_all(tgt_out, to_send)


def place(*refs):
    sources, places, sems = refs[0:4], refs[4:8], refs[8]
    copies = [
        pltpu.make_async_copy(src, dst, sems.at[i])
        for i, (src, dst) in enumerate(zip(sources, places))
    ]
    for copy in copies:
        copy.start()
    for copy in copies:
        copy.wait()


def local(src_feats, src_factor, tgt_feats, tgt_factor, rank_weight):
    n_src = lax.axis_size("src")
    n_tgt = lax.axis_size("tgt")
    low = 2 if n_tgt % 2 == 0 else 1
    n_a, n_b = n_src * low, n_tgt // low
    f, rows = src_feats.shape
    k = src_factor.shape[0]
    cols = tgt_feats.shape[1]
    stack = f + AUG + k
    split = (rows // 2 + 15) // 16 * 16
    f32, bf16 = jnp.float32, jnp.bfloat16
    scale = 1.0 / (cols * n_src * n_tgt)
    vmem = pl.BlockSpec(memory_space=pltpu.VMEM)
    hbm = pl.BlockSpec(memory_space=pltpu.HBM)
    dma = pltpu.SemaphoreType.DMA
    out_shape = (
        jax.ShapeDtypeStruct((f, rows), f32),
        jax.ShapeDtypeStruct((k, rows), f32),
        jax.ShapeDtypeStruct((f, cols), f32),
        jax.ShapeDtypeStruct((k, cols), f32),
    )
    results = pl.pallas_call(
        functools.partial(kernel, n_src, n_tgt, low, scale),
        out_shape=tuple(pltpu.VMEM(o.shape, o.dtype) for o in out_shape),
        in_specs=[hbm] * 5,
        out_specs=(vmem,) * 4,
        scratch_shapes=[
            pltpu.VMEM((f, rows), bf16),
            pltpu.VMEM((k, rows), bf16),
            pltpu.VMEM((f, cols), bf16),
            pltpu.VMEM((k, cols), bf16),
            pltpu.VMEM((1, k), f32),
            pltpu.VMEM((n_a, split, 2 * stack), bf16),
            pltpu.VMEM((n_b, stack, cols), bf16),
            pltpu.VMEM((n_a * rows, stack), bf16),
            pltpu.VMEM((stack, n_a * rows), bf16),
            pltpu.VMEM((n_a * rows, stack), f32),
            pltpu.VMEM((n_a, rows // 2, 2 * stack), f32),
            pltpu.VMEM((n_a, rows // 2, 2 * stack), f32),
            pltpu.VMEM((n_b, f + k, cols), f32),
            pltpu.VMEM((n_b, f + k, cols), f32),
            dma((5,)),
            dma((n_a,)),
            dma((n_a,)),
            dma((n_b,)),
            dma((n_b,)),
            dma((n_a,)),
            dma((n_a,)),
            dma((n_b,)),
            dma((n_b,)),
        ],
        compiler_params=pltpu.CompilerParams(
            collective_id=0, has_side_effects=True, vmem_limit_bytes=63 * 1024 * 1024
        ),
    )(src_feats, src_factor, tgt_feats, tgt_factor, rank_weight.reshape(1, k))
    return pl.pallas_call(
        place,
        out_shape=out_shape,
        in_specs=[vmem] * 4,
        out_specs=(hbm,) * 4,
        scratch_shapes=[dma((4,))],
    )(*(pltpu.with_memory_space_constraint(r, pltpu.VMEM) for r in results))


def solution(mesh):
    src = P(None, ("src", "tgt"))
    tgt = P(None, ("tgt", "src"))
    return jax.shard_map(
        local,
        mesh=mesh,
        in_specs=(src, src, tgt, tgt, P()),
        out_specs=(src, src, tgt, tgt),
        check_vma=False,
    )
```

```python
import functools

import jax
import jax.numpy as jnp
from jax import lax
from jax.experimental import pallas as pl
from jax.experimental.pallas import tpu as pltpu
from jax.sharding import PartitionSpec as P

MESH = pl.DeviceIdType.MESH
NT = (((1,), (1,)), ((), ()))
AUG = 16


def each(low, high, body):
    if high - low <= 8:
        for i in range(low, high):
            body(i)
    else:
        lax.fori_loop(low, high, lambda i, c: (body(i), c)[1], 0)


def fold(low, high, start, body):
    if high - low <= 8:
        for i in range(low, high):
            start = body(i, start)
        return start
    return lax.fori_loop(low, high, body, start)


def split3(value):
    high = value.astype(jnp.bfloat16).astype(jnp.float32)
    rest = value - high
    mid = rest.astype(jnp.bfloat16).astype(jnp.float32)
    return high, mid, rest - mid


def aug_rows(feats, first, ones_at, extra):
    norm = jnp.sum(feats * feats, axis=0, keepdims=True) + extra
    high, mid, low = split3(norm)
    shape = (AUG, feats.shape[1])
    row = lax.broadcasted_iota(jnp.int32, shape, 0)
    out = jnp.where((row >= ones_at) & (row < ones_at + 3), 1.0, 0.0)
    for k, part in enumerate((high, mid, low)):
        out = jnp.where(row == first + k, jnp.broadcast_to(part, shape), out)
    return out


def kernel(
    n_src, n_tgt, low, scale,
    x_hbm, q_hbm, y_hbm, r_hbm, g_hbm,
    gx_ref, gq_ref, gy_ref, gr_ref,
    x_in, q_in, y_in, r_in, g_in,
    a_slots, t_slots, row_stack, col_stack, row_acc, last_terms,
    src_out, src_in, tgt_out, tgt_in,
    load_sem, a_send, a_recv, t_send, t_recv, so_send, so_recv, to_send, to_recv,
):
    f, rows = x_in.shape
    k = q_in.shape[0]
    head = f + AUG
    stack = head + k
    half = rows // 2
    split = a_slots.shape[1]
    n_a = n_src * low
    n_b = n_tgt // low
    me_s = lax.axis_index("src")
    me_t = lax.axis_index("tgt")
    me_b = me_t // low
    me_low = me_t % low
    me_a = me_s * low + me_low

    def a_peer(d):
        return lax.rem(me_a + d, n_a)

    def b_peer(d):
        if n_b & (n_b - 1) or n_b > 8:
            return lax.rem(me_b + d, n_b)
        peer, bit = me_b, 1
        while bit <= d:
            if d & bit:
                peer = peer + bit - 2 * bit * ((peer // bit) % 2)
            bit *= 2
        return peer

    def a_device(a):
        return {"src": a // low, "tgt": me_b * low + a % low}

    def b_device(b):
        return {"src": me_s, "tgt": b * low + me_low}

    loads = [
        pltpu.make_async_copy(src, dst, load_sem.at[i])
        for i, (src, dst) in enumerate(
            ((x_hbm, x_in), (q_hbm, q_in), (y_hbm, y_in), (r_hbm, r_in), (g_hbm, g_in))
        )
    ]
    barrier = pltpu.get_barrier_semaphore()

    def greet(device):
        pl.semaphore_signal(barrier, inc=1, device_id=device, device_id_type=MESH)

    each(1, n_a, lambda d: greet(a_device(a_peer(d))))
    each(1, n_b, lambda d: greet(b_device(b_peer(d))))

    for load in loads:
        load.start()

    for load in loads:
        load.wait()

    x = x_in[...].astype(jnp.float32)
    mine = jnp.concatenate([x * -2.0, aug_rows(x, 0, 3, 0.0), q_in[...].astype(jnp.float32)], 0)
    mine = mine.T.astype(jnp.bfloat16)
    a_slots[me_a, :, 0:stack] = mine[0:split]
    a_slots[me_a, 0 : rows - split, stack : 2 * stack] = mine[split:]
    inv_row = 1.0 / g_in[...]
    square = (k, k)
    diagonal = lax.broadcasted_iota(jnp.int32, square, 0) == lax.broadcasted_iota(
        jnp.int32, square, 1
    )
    inverse_g = jnp.sum(
        jnp.where(diagonal, jnp.broadcast_to(inv_row, square), 0.0), axis=1, keepdims=True
    )
    y = y_in[...]
    t_slots[me_b, 0:f, :] = y
    t_slots[me_b, f:head, :] = aug_rows(y.astype(jnp.float32), 3, 0, 1.0).astype(jnp.bfloat16)
    t_slots[me_b, head:, :] = (r_in[...].astype(jnp.float32) * inverse_g).astype(jnp.bfloat16)

    pl.semaphore_wait(barrier, n_a + n_b - 2)

    def remote(src, dst, send, recv, device):
        return pltpu.make_async_remote_copy(
            src_ref=src, dst_ref=dst, send_sem=send, recv_sem=recv,
            device_id=device, device_id_type=MESH,
        )

    def wait_all(slots, sem):
        ref = slots.at[pl.ds(0, slots.shape[0] - 1)]
        pltpu.make_async_copy(ref, ref, sem.at[0]).wait()

    def a_copy(d, slot):
        ref = a_slots.at[slot]
        return remote(ref, ref, a_send.at[0], a_recv.at[0], a_device(a_peer(d)))

    def t_copy(d, slot):
        ref = t_slots.at[slot]
        return remote(ref, ref, t_send.at[0], t_recv.at[slot], b_device(b_peer(d)))

    def so_copy(a):
        return remote(
            src_out.at[a], src_in.at[me_a], so_send.at[0], so_recv.at[0], a_device(a)
        )

    def to_copy(d, slot):
        return remote(
            tgt_out.at[d], tgt_in.at[slot], to_send.at[0], to_recv.at[0], b_device(b_peer(d))
        )

    each(1, n_a, lambda d: a_copy(d, me_a).start())
    each(1, n_b, lambda d: t_copy(d, me_b).start())

    wait_all(a_slots, a_recv)
    for a in range(n_a):
        row_stack[a * rows : a * rows + split, :] = a_slots[a, :, 0:stack]
        row_stack[a * rows + split : (a + 1) * rows, :] = a_slots[
            a, 0 : rows - split, stack : 2 * stack
        ]
    col_stack[...] = row_stack[...].T

    def right_side(several):
        parts = []
        for d in several:
            peer = b_peer(d)
            if not (isinstance(d, int) and d == 0):
                t_copy(d, peer).wait_recv()
            parts.append(t_slots[peer])
        cols = parts[0].shape[1]
        zero_low = jnp.zeros((head, cols), jnp.bfloat16)
        zero_high = jnp.zeros((k, cols), jnp.bfloat16)
        rhs = jnp.concatenate(
            [jnp.concatenate([p[0:head], zero_high], 0) for p in parts]
            + [jnp.concatenate([zero_low, p[head:]], 0) for p in parts],
            1,
        )
        return parts, rhs

    def pair_terms(points, rhs):
        wide = rhs.shape[1] // 2
        both = jnp.dot(points, rhs, preferred_element_type=jnp.float32)
        squared, plan = both[:, 0:wide], both[:, wide:]
        inv = lax.rsqrt(squared)
        return jnp.concatenate(
            [(plan * inv).astype(jnp.bfloat16), (squared * inv).astype(jnp.bfloat16)], 1
        )

    def row_sums(terms, rhs):
        return lax.dot_general(terms, rhs, NT, preferred_element_type=jnp.float32)

    def put_cols(several, parts, terms):
        col = jnp.dot(col_stack[...], terms, preferred_element_type=jnp.float32)
        cols = parts[0].shape[1]
        wide = cols * len(parts)
        for i, d in enumerate(several):
            at = slice(i * cols, (i + 1) * cols)
            mass = col[f + 3 : f + 4, at]
            tgt_out[d, 0:f, :] = parts[i][0:f].astype(jnp.float32) * mass + 0.5 * col[0:f, at]
            tgt_out[d, f:, :] = col[head:, wide + i * cols : wide + (i + 1) * cols]
            if not (isinstance(d, int) and d == 0):
                to_copy(d, me_b).start()

    size = next(n for n in (4, 2, 1) if n_b % n == 0)
    groups = n_b // size

    def earlier(g):
        several = [g * size + i for i in range(size)]
        parts, rhs = right_side(several)
        terms = pair_terms(row_stack[...], rhs)
        put_cols(several, parts, terms)
        row_acc[...] += row_sums(terms, rhs)

    if groups > 1:
        row_acc[...] = jnp.zeros_like(row_acc)
        each(1, groups, earlier)

    several = list(range(size))
    parts, rhs = right_side(several)
    piece = n_a // 2 if n_a % 2 == 0 else n_a
    pieces = n_a // piece
    for c in reversed(range(pieces)):
        base = lax.rem(me_a // piece + c, pieces) * piece
        at = pl.ds(pl.multiple_of(base * rows, 16), piece * rows)
        terms = pair_terms(row_stack[at, :], rhs)
        last_terms[at, :] = terms
        row = row_sums(terms, rhs)
        if groups > 1:
            row = row + row_acc[at, :]
        for i in range(piece):
            a = base + i
            src_out[a, :, 0:stack] = row[i * rows : i * rows + half]
            src_out[a, :, stack : 2 * stack] = row[i * rows + half : (i + 1) * rows]

            @pl.when(a != me_a)
            def _():
                so_copy(a).start()

    put_cols(several, parts, last_terms[...])

    wait_all(tgt_in, to_recv)
    total = fold(1, n_b, tgt_out[0], lambda d, sum_: sum_ + tgt_in[b_peer(d)])
    gy_ref[...] = total[0:f] * scale
    gr_ref[...] = total[f:] * inverse_g * scale

    wait_all(src_in, so_recv)
    total = fold(1, n_a, src_out[me_a], lambda d, sum_: sum_ + src_in[a_peer(d)])
    total = jnp.concatenate([total[:, 0:stack], total[:, stack : 2 * stack]], 0).T
    gx_ref[...] = (x * total[f : f + 1] - total[0:f]) * scale
    gq_ref[...] = total[head:] * scale

    wait_all(a_slots, a_send)
    wait_all(t_slots, t_send)
    wait_all(src_out, so_send)
    wait_all(tgt_out, to_send)


def place(*refs):
    sources, places, sems = refs[0:4], refs[4:8], refs[8]
    copies = [
        pltpu.make_async_copy(src, dst, sems.at[i])
        for i, (src, dst) in enumerate(zip(sources, places))
    ]
    for copy in copies:
        copy.start()
    for copy in copies:
        copy.wait()


def local(src_feats, src_factor, tgt_feats, tgt_factor, rank_weight):
    n_src = lax.axis_size("src")
    n_tgt = lax.axis_size("tgt")
    low = 2 if n_tgt % 2 == 0 else 1
    n_a, n_b = n_src * low, n_tgt // low
    f, rows = src_feats.shape
    k = src_factor.shape[0]
    cols = tgt_feats.shape[1]
    stack = f + AUG + k
    split = (rows // 2 + 15) // 16 * 16
    f32, bf16 = jnp.float32, jnp.bfloat16
    scale = 1.0 / (cols * n_src * n_tgt)
    vmem = pl.BlockSpec(memory_space=pltpu.VMEM)
    hbm = pl.BlockSpec(memory_space=pltpu.HBM)
    dma = pltpu.SemaphoreType.DMA
    out_shape = (
        jax.ShapeDtypeStruct((f, rows), f32),
        jax.ShapeDtypeStruct((k, rows), f32),
        jax.ShapeDtypeStruct((f, cols), f32),
        jax.ShapeDtypeStruct((k, cols), f32),
    )
    results = pl.pallas_call(
        functools.partial(kernel, n_src, n_tgt, low, scale),
        out_shape=tuple(pltpu.VMEM(o.shape, o.dtype) for o in out_shape),
        in_specs=[hbm] * 5,
        out_specs=(vmem,) * 4,
        scratch_shapes=[
            pltpu.VMEM((f, rows), bf16),
            pltpu.VMEM((k, rows), bf16),
            pltpu.VMEM((f, cols), bf16),
            pltpu.VMEM((k, cols), bf16),
            pltpu.VMEM((1, k), f32),
            pltpu.VMEM((n_a, split, 2 * stack), bf16),
            pltpu.VMEM((n_b, stack, cols), bf16),
            pltpu.VMEM((n_a * rows, stack), bf16),
            pltpu.VMEM((stack, n_a * rows), bf16),
            pltpu.VMEM((n_a * rows, stack), f32),
            pltpu.VMEM((n_a * rows, 2 * cols * next(n for n in (4, 2, 1) if n_b % n == 0)), bf16),
            pltpu.VMEM((n_a, rows // 2, 2 * stack), f32),
            pltpu.VMEM((n_a, rows // 2, 2 * stack), f32),
            pltpu.VMEM((n_b, f + k, cols), f32),
            pltpu.VMEM((n_b, f + k, cols), f32),
            dma((5,)),
            dma((n_a,)),
            dma((n_a,)),
            dma((n_b,)),
            dma((n_b,)),
            dma((n_a,)),
            dma((n_a,)),
            dma((n_b,)),
            dma((n_b,)),
        ],
        compiler_params=pltpu.CompilerParams(
            collective_id=0, has_side_effects=True, vmem_limit_bytes=63 * 1024 * 1024
        ),
    )(src_feats, src_factor, tgt_feats, tgt_factor, rank_weight.reshape(1, k))
    return pl.pallas_call(
        place,
        out_shape=out_shape,
        in_specs=[vmem] * 4,
        out_specs=(hbm,) * 4,
        scratch_shapes=[dma((4,))],
    )(*(pltpu.with_memory_space_constraint(r, pltpu.VMEM) for r in results))


def solution(mesh):
    src = P(None, ("src", "tgt"))
    tgt = P(None, ("tgt", "src"))
    return jax.shard_map(
        local,
        mesh=mesh,
        in_specs=(src, src, tgt, tgt, P()),
        out_specs=(src, src, tgt, tgt),
        check_vma=False,
    )
```
